128 devices in a mesh: row: 16 (over x, z_lo, core), col: 8 (over z_hi, y).
Axes of the slice: x: 4, y: 4, z: 4 (z_hi: 2, z_lo: 2; z = z_hi * 2 + z_lo), core: 2. Of those that a mesh axis runs over, the one named last changes fastest.
Arguments:
- amplitudes: bfloat16 [3, 1024, 16384], P(None, 'row', 'col'), may hold values from -6 to 6
- integrals: bfloat16 [5, 16384, 16384], P(None, 'col', 'row'), may hold values from -0.046875 to 0.046875
- tile_pairs: int32 [5, 2], replicated, may hold values from 0 to 2, as said below
- driving: bfloat16 [3, 1024, 16384], P(None, 'col', 'row'), may hold values from -6 to 6
- occupied_energy: float32 [32], replicated, may hold values from -1 to -0.2
- virtual_energy: float32 [3, 2, 128], replicated, may hold values from 0.3 to 2
Outputs:
- residual: float32 [3, 1024, 16384], P(None, 'col', 'row')
- update: float32 [3, 1024, 16384], P(None, 'col', 'row')
The draws below stay inside these ranges and needn't reach their ends.
Inputs may be any that keep to these rules, and one draw needn't show every extreme that they name: `tile_pairs`: the 3 tiles fall into two symmetry sectors, two tiles in one and one in the other; each ordered pair of tiles within a sector is one row, in an order drawn from the seed.
All inputs are finite; a program needn't handle non-finite values.
Results may differ from the reference program's by a relative error of at most 0.0003.
Values may be sent and summed in bfloat16 or wider, within the bound.
A program may use at most 192 MiB of HBM per device.

```python
import jax
import jax.numpy as jnp
from jax import lax

NO = 32
BW = 128
NTILE = 3
NWT = 5
PAIRS = 1024
QT = 16384


def draw_tile_pairs(key, part):
    key = jax.random.fold_in(key, 11)
    role_key, order_key = jax.random.split(key)
    roles = jax.random.permutation(role_key, 3)
    first_tile = roles[0]
    second_tile = roles[1]
    lone_tile = roles[2]
    listed = jnp.stack([jnp.stack([first_tile, first_tile]), jnp.stack([first_tile, second_tile]), jnp.stack([second_tile, first_tile]), jnp.stack([second_tile, second_tile]), jnp.stack([lone_tile, lone_tile])])
    order = jax.random.permutation(order_key, 5)
    return listed[order].astype(jnp.int32)


def block_scale(own_key, dims, cuts, least, largest):
    gain = 1.0
    for position, parts in cuts:
        draws = jax.random.uniform(jax.random.fold_in(jax.random.fold_in(own_key, 6), position), (parts,), jnp.float32, least / len(cuts), largest / len(cuts))
        gain = gain * jnp.repeat(jnp.exp(draws), dims[position] // parts).reshape((-1,) + (1,) * (len(dims) - 1 - position))
    return gain


def noise(rng, shape, scale, bound, cuts=(), kind=jnp.bfloat16):
    values = scale * jax.random.normal(rng, shape, jnp.float32)
    if cuts:
        values = values * block_scale(rng, shape, cuts, -0.22, 0.18)
    return jnp.clip(values, -bound, bound).astype(kind)


def setup_inputs(seed: int = 0) -> dict:
    key_of = jax.random.split(jax.random.key(seed), 7)
    return {
        "amplitudes": noise(key_of[0], (NTILE, PAIRS, QT), 1.0, 6.0, ((1, 16), (2, 8))),
        "integrals": noise(key_of[1], (NWT, QT, QT), QT ** -0.5, 0.046875, ((1, 8), (2, 16))),
        "tile_pairs": draw_tile_pairs(jax.random.fold_in(key_of[6], 71), 0),
        "driving": noise(key_of[3], (NTILE, PAIRS, QT), 1.0, 6.0, ((1, 8), (2, 16))),
        "occupied_energy": jnp.clip(jax.random.uniform(key_of[4], (NO,), jnp.float32, -1.0, -0.2), -1.0, -0.2),
        "virtual_energy": jnp.clip(jax.random.uniform(key_of[5], (NTILE, 2, BW), jnp.float32, 0.3, 2.0), 0.3, 2.0),
    }


def reference(amplitudes, integrals, tile_pairs, driving, occupied_energy, virtual_energy):
    tile_ids = jnp.arange(NTILE, dtype=jnp.int32)
    ladder = jnp.zeros((NTILE, NO * NO, BW * BW), jnp.float32)
    for entry in range(NWT):
        selected = lax.dynamic_index_in_dim(amplitudes, tile_pairs[entry, 0].astype(jnp.int32), 0, keepdims=False)
        product = jnp.dot(selected, integrals[entry], preferred_element_type=jnp.float32)
        mirrored = product.reshape(NO, NO, BW * BW).transpose(1, 0, 2).reshape(NO * NO, BW * BW)
        chosen = (tile_ids == tile_pairs[entry, 1])[:, None, None]
        ladder = ladder + jnp.where(chosen, (product + mirrored)[None], jnp.float32(0.0))
    residual = driving.astype(jnp.float32) + ladder
    pair_energy = (occupied_energy[:, None] + occupied_energy[None, :]).reshape(NO * NO)
    virtual_pair = (virtual_energy[:, 0, :, None] + virtual_energy[:, 1, None, :]).reshape(NTILE, BW * BW)
    denominator = pair_energy[None, :, None] - virtual_pair[:, None, :]
    return residual, residual / denominator
```

```python
import functools

import jax
import jax.numpy as jnp
from jax import lax
from jax.experimental import pallas as pl
from jax.experimental.pallas import tpu as pltpu
from jax.sharding import PartitionSpec as P

MESH = pl.DeviceIdType.MESH
NB = 8
QN = 256
RN = 4
ROUNDS = 12
SET = 144
HALF = SET // 2


def kernel(
    tp_ref, amp_ref, int_hbm, lad_ref,
    g, wt, s_buf, t, fwd, rcv, zr, f, xr,
    int_sem, z_sem, x_sem, f_sem, t_sem, fwd_sem, rcv_sem, zr_sem, xr_sem,
):
    row, col = lax.axis_index("row"), lax.axis_index("col")
    x, zl, k = row // 4, (row // 2) % 2, row % 2
    zh, y = col // 4, col % 4

    def at_row(xx, zz, kk):
        return (xx * 4 + zz * 2 + kk, col)

    def at_col(cc):
        return (row, cc)

    xp, xm, xo = (x + 1) % 4, (x + 3) % 4, (x + 2) % 4
    yp, ym, yo = (y + 1) % 4, (y + 3) % 4, (y + 2) % 4
    right, left = at_row(xp, zl, k), at_row(xm, zl, k)
    zpart, twin = at_row(x, 1 - zl, k), at_row(x, zl, 1 - k)
    up, down = at_col(zh * 4 + yp), at_col(zh * 4 + ym)
    far = at_col((1 - zh) * 4 + y)

    loads = [pltpu.make_async_copy(int_hbm.at[e], wt.at[e], int_sem.at[e]) for e in range(5)]
    for c in loads:
        c.start()

    barrier = pltpu.get_barrier_semaphore()
    partners = [right, left, zpart, twin] + [at_col((col + d) % NB) for d in range(1, NB)]
    for p in partners:
        pl.semaphore_signal(barrier, inc=1, device_id=p, device_id_type=MESH)

    src = [tp_ref[2 * e] for e in range(5)]
    dst = [tp_ref[2 * e + 1] for e in range(5)]
    counts = [sum((src[e] == v).astype(jnp.int32) for e in range(5)) for v in range(3)]
    lone = jnp.where(counts[0] == 1, 0, jnp.where(counts[1] == 1, 1, 2))
    first = jnp.where(lone == 0, 1, 0)
    second = jnp.where(lone == 2, 1, 2)

    def entry(a, b):
        found = jnp.int32(0)
        for e in range(1, 5):
            found = jnp.where((src[e] == a) & (dst[e] == b), e, found)
        return found

    e_l = entry(lone, lone)
    e_ff, e_sf = entry(first, first), entry(second, first)
    e_fs, e_ss = entry(first, second), entry(second, second)

    own = x * 2 + zl
    for s, tile in enumerate((lone, first, second)):
        g[s, own, k] = amp_ref[tile]
    pl.semaphore_wait(barrier, len(partners))

    def rdma(ref_src, ref_dst, ss, rs, dev):
        return pltpu.make_async_remote_copy(
            src_ref=ref_src, dst_ref=ref_dst, send_sem=ss, recv_sem=rs, device_id=dev, device_id_type=MESH
        )

    def chip(xx, zz):
        return xx * 2 + zz

    def cz(s, a):
        return rdma(g.at[s, a, k], g.at[s, a, k], z_sem.at[0, s], z_sem.at[1, s], zpart)

    def cx(s, a, side, which):
        return rdma(
            g.at[s, a, k], g.at[s, a, k], x_sem.at[0, s, side, which], x_sem.at[1, s, side, which],
            right if side == 0 else left,
        )

    def cf(s, a, side, which):
        part = g.at[s, a, k, pl.ds(32 * side, 32)]
        return rdma(part, part, f_sem.at[0, s, side, which], f_sem.at[1, s, side, which], right if side == 0 else left)

    def ct(s, a, i, kk=None):
        kk = k if kk is None else kk
        return rdma(g.at[s, a, kk], g.at[s, a, kk], t_sem.at[0, s, i], t_sem.at[1, s, i], twin)

    own_z = chip(x, 1 - zl)
    lefts, rights = (chip(xm, zl), chip(xm, 1 - zl)), (chip(xp, zl), chip(xp, 1 - zl))
    fars = (chip(xo, zl), chip(xo, 1 - zl))
    order = (own, own_z, *lefts, *rights, *fars)

    def send_own_z(s):
        cz(s, own).start()

    def send_own_x(s):
        cx(s, own, 0, 0).start()
        cx(s, own, 1, 0).start()
        ct(s, own, 0).start()

    def pass_z(s):
        cz(s, own_z).wait_recv()
        cx(s, own_z, 0, 1).start()
        cx(s, own_z, 1, 1).start()
        ct(s, own_z, 1).start()

    def pass_x(s, which):
        cx(s, lefts[which], 0, which).wait_recv()
        cf(s, lefts[which], 0, which).start()
        ct(s, lefts[which], 2 + which).start()
        cx(s, rights[which], 1, which).wait_recv()
        cf(s, rights[which], 1, which).start()
        ct(s, rights[which], 4 + which).start()

    def pass_far(s):
        for which in range(2):
            cf(s, fars[which], 0, which).wait_recv()
            cf(s, fars[which], 1, which).wait_recv()
            ct(s, fars[which], 6 + which).start()

    def end_twin(s):
        for i, a in enumerate(order):
            ct(s, a, i, 1 - k).wait_recv()

    def end_sends(s):
        cz(s, own).wait_send()
        for side in range(2):
            cx(s, own, side, 0).wait_send()
            cx(s, own_z, side, 1).wait_send()
            for which in range(2):
                cf(s, (lefts, rights)[side][which], side, which).wait_send()
        for i, a in enumerate(order):
            ct(s, a, i).wait_send()

    def c_fwd(r, side):
        return rdma(
            t.at[r, 0, pl.ds(HALF * side, HALF)], fwd.at[r, side],
            fwd_sem.at[0, r, side], fwd_sem.at[1, r, side], up if side == 0 else down,
        )

    def c_rcv(r, side):
        return rdma(
            t.at[r, 1 + side], rcv.at[r, side],
            rcv_sem.at[0, r, side], rcv_sem.at[1, r, side], up if side == 0 else down,
        )

    def c_zr(r):
        start = pl.multiple_of(64 * (1 - zh), 8)
        return rdma(t.at[r, 3, pl.ds(start, 80)], zr.at[r], zr_sem.at[0, r], zr_sem.at[1, r], far)

    def c_xr(r, d):
        return rdma(f.at[r, d], xr.at[r, d - 1], xr_sem.at[0, r, d - 1], xr_sem.at[1, r, d - 1], at_col((col + d) % NB))

    def make_block(c, d):
        b = (c + d) % NB
        direct = s_buf[c, :, b]
        if d == 0:
            return direct
        other = s_buf[b, :, c]
        mirrored = jnp.stack(
            [
                jnp.concatenate([other[0, :4], other[1, :4]], axis=0),
                jnp.concatenate([other[0, 4:], other[1, 4:]], axis=0),
            ]
        )
        return direct + mirrored

    def stage1(r, pairs):
        n = r % RN
        columns = pl.ds(pl.multiple_of(n * QN, QN), QN)
        for m in range(4):
            total = None
            for slot, e in pairs:
                lhs = g[slot, 2 * m : 2 * m + 2].reshape(256, 2048)
                part = jnp.dot(lhs, wt[e, :, columns], preferred_element_type=jnp.float32)
                total = part if total is None else total + part
            s_buf[2 * m : 2 * m + 2] = total.reshape(2, 2, 8, 8, QN)
        for rel, yy in enumerate((yo, yp, ym, y)):
            at = 0
            for zz in range(2):
                for d in range(5 - zz):
                    t[r, rel, pl.ds(at, 16)] = make_block(zz * 4 + yy, d).reshape(16, QN)
                    at += 16
            if rel == 0:
                c_fwd(r, 0).start()
                c_fwd(r, 1).start()

    def stage2(r):
        for side in range(2):
            rows = pl.ds(HALF * side, HALF)
            c_fwd(r, side).wait_recv()
            t[r, 1 + side, rows] = t[r, 1 + side, rows] + fwd[r, side]
            c_rcv(r, side).start()

    def stage3(r):
        c_rcv(r, 0).wait_recv()
        c_rcv(r, 1).wait_recv()
        t[r, 3] = t[r, 3] + rcv[r, 0] + rcv[r, 1]
        c_zr(r).start()

    def stage4(r):
        c_zr(r).wait_recv()
        mine = pl.ds(pl.multiple_of(80 * zh, 8), 64)
        theirs = pl.ds(pl.multiple_of(16 * zh, 8), 64)
        f[r, 0:4] = (t[r, 3, mine] + zr[r, theirs]).reshape(4, 16, QN)
        f[r, 4] = t[r, 3, pl.ds(64, 16)] + zr[r, pl.ds(64, 16)]
        for d in range(1, 4):
            c_xr(r, d).start()

        @pl.when(zh == 0)
        def _():
            c_xr(r, 4).start()

    def stage5(r):
        for d in range(1, 4):
            c_xr(r, d).wait_recv()

        @pl.when(zh == 1)
        def _():
            c_xr(r, 4).wait_recv()

        s, n = r // RN, r % RN
        columns = pl.ds(pl.multiple_of(n * QN, QN), QN)

        def place(block, b, swap):
            for i in range(4):
                for j in range(4):
                    p, q = (j, i) if swap else (i, j)
                    at = (p // 2) * 8 + (q // 2) * 4 + (p % 2) * 2 + q % 2
                    lad_ref[s, pl.ds(i * 32 + b * 4 + j, 1), columns] = block(at)

        def from_f(d):
            return lambda at: f[r, d, pl.ds(at, 1)]

        def from_xr(d):
            return lambda at: xr[r, d - 1, pl.ds(at, 1)]

        def at_of(p, q):
            return (p // 2) * 8 + (q // 2) * 4 + (p % 2) * 2 + q % 2

        for i in range(4):
            for j in range(4):
                lad_ref[s, pl.ds(i * 32 + col * 4 + j, 1), columns] = (
                    f[r, 0, pl.ds(at_of(i, j), 1)] + f[r, 0, pl.ds(at_of(j, i), 1)]
                )
        for d in range(1, 4):
            place(from_f(d), (col + d) % NB, False)
            place(from_xr(d), (col + NB - d) % NB, True)

        @pl.when(zh == 0)
        def _():
            place(from_f(4), (col + 4) % NB, False)

        @pl.when(zh == 1)
        def _():
            place(from_xr(4), (col + 4) % NB, True)

    def run(lo, hi, first_stage):
        def step(it, carry):
            @pl.when(it < hi)
            def _():
                first_stage(it)

            for lag, stage in ((1, stage2), (2, stage3), (3, stage4), (4, stage5)):
                @pl.when((it - lag >= lo) & (it - lag < hi))
                def _(lag=lag, stage=stage):
                    stage(it - lag)

            return carry

        lax.fori_loop(lo, hi + 4, step, 0)

    send_own_z(0)
    send_own_x(0)
    pass_z(0)
    send_own_z(1)
    send_own_z(2)
    pass_x(0, 0)
    pass_x(0, 1)
    pass_far(0)
    for s in (1, 2):
        send_own_x(s)
        pass_z(s)
    for c in loads:
        c.wait()
    end_twin(0)
    run(0, RN, lambda r: stage1(r, [(0, e_l)]))
    for s in (1, 2):
        pass_x(s, 0)
        pass_x(s, 1)
    for s in (1, 2):
        pass_far(s)
    for s in (1, 2):
        end_twin(s)

    def later(r):
        one = r < 2 * RN
        stage1(r, [(1, jnp.where(one, e_ff, e_fs)), (2, jnp.where(one, e_sf, e_ss))])

    run(RN, 3 * RN, later)

    for s in range(3):
        end_sends(s)

    def drain(r, carry):
        for side in range(2):
            c_fwd(r, side).wait_send()
            c_rcv(r, side).wait_send()
        c_zr(r).wait_send()
        for d in range(1, 4):
            c_xr(r, d).wait_send()

        @pl.when(zh == 0)
        def _():
            c_xr(r, 4).wait_send()

        return carry

    lax.fori_loop(0, ROUNDS, drain, 0)


def ladder_call(tile_pairs, amplitudes, integrals):
    dma = pltpu.SemaphoreType.DMA
    return pl.pallas_call(
        kernel,
        out_shape=jax.ShapeDtypeStruct((3, 128, 1024), jnp.float32),
        in_specs=[
            pl.BlockSpec(memory_space=pltpu.SMEM),
            pl.BlockSpec(memory_space=pltpu.VMEM),
            pl.BlockSpec(memory_space=pl.ANY),
        ],
        out_specs=pl.BlockSpec(memory_space=pltpu.VMEM),
        scratch_shapes=[
            pltpu.VMEM((3, NB, 2, 64, 2048), jnp.bfloat16),
            pltpu.VMEM((5, 2048, 1024), jnp.bfloat16),
            pltpu.VMEM((NB, 2, NB, 8, QN), jnp.float32),
            pltpu.VMEM((ROUNDS, 4, SET, QN), jnp.float32),
            pltpu.VMEM((ROUNDS, 2, HALF, QN), jnp.float32),
            pltpu.VMEM((ROUNDS, 2, SET, QN), jnp.float32),
            pltpu.VMEM((ROUNDS, 80, QN), jnp.float32),
            pltpu.VMEM((ROUNDS, 5, 16, QN), jnp.float32),
            pltpu.VMEM((ROUNDS, 4, 16, QN), jnp.float32),
            dma((5,)),
            dma((2, 3)),
            dma((2, 3, 2, 2)),
            dma((2, 3, 2, 2)),
            dma((2, 3, 8)),
            dma((2, ROUNDS, 2)),
            dma((2, ROUNDS, 2)),
            dma((2, ROUNDS)),
            dma((2, ROUNDS, 4)),
        ],
        compiler_params=pltpu.CompilerParams(
            collective_id=0, has_side_effects=True, vmem_limit_bytes=60 << 20
        ),
        cost_estimate=pl.CostEstimate(flops=21_474_836_480, bytes_accessed=24 << 20, transcendentals=0),
    )(tile_pairs, amplitudes, integrals)


def body(amplitudes, integrals, tile_pairs, driving, occupied_energy, virtual_energy):
    tile_count, row_count, tile_width = driving.shape
    occupied = occupied_energy.shape[0]
    block_width = virtual_energy.shape[2]
    row, col = lax.axis_index("row"), lax.axis_index("col")

    own = row // 2
    pieces = amplitudes.reshape(tile_count, 2, NB, 2, 2, -1)
    distance = (jnp.arange(NB) - own) % NB
    direct = (distance < 4) | ((distance == 4) & (own < 4))
    ordered = jnp.where(
        direct[None, :, None, None, None, None],
        pieces.transpose(0, 2, 3, 1, 4, 5),
        pieces.transpose(0, 2, 3, 4, 1, 5),
    ).reshape(amplitudes.shape)
    by_slot = ladder_call(tile_pairs.reshape(-1), ordered, integrals)

    counts = (tile_pairs[:, 0][None, :] == jnp.arange(tile_count)[:, None]).sum(1)
    lone = jnp.argmin(counts)
    tile = jnp.arange(tile_count)
    slot = jnp.where(tile == lone, 0, 1 + tile - (tile > lone))
    ladder = jnp.stack(
        [lax.dynamic_index_in_dim(by_slot, slot[v], 0, keepdims=False) for v in range(tile_count)]
    )
    residual = driving.astype(jnp.float32) + ladder
    pair_energy = (occupied_energy[:, None] + occupied_energy[None, :]).reshape(occupied * occupied)
    pair_energy = lax.dynamic_slice_in_dim(pair_energy, col * row_count, row_count)
    block_count = tile_width // block_width
    leading = lax.dynamic_slice_in_dim(virtual_energy[:, 0, :], row * block_count, block_count, 1)
    virtual_pair = (leading[:, :, None] + virtual_energy[:, 1, None, :]).reshape(tile_count, tile_width)
    denominator = pair_energy[None, :, None] - virtual_pair[:, None, :]
    return (residual, residual / denominator)


def solution(mesh):
    return jax.shard_map(
        body,
        mesh=mesh,
        in_specs=(
            P(None, "row", "col"),
            P(None, "col", "row"),
            P(),
            P(None, "col", "row"),
            P(),
            P(),
        ),
        out_specs=(P(None, "col", "row"), P(None, "col", "row")),
        check_vma=False,
    )
```

```python
import functools

import jax
import jax.numpy as jnp
from jax import lax
from jax.experimental import pallas as pl
from jax.experimental.pallas import tpu as pltpu
from jax.sharding import PartitionSpec as P

MESH = pl.DeviceIdType.MESH
NB = 8
QN = 256
RN = 4
ROUNDS = 12
SET = 144
HALF = 80
WIDE = QN + QN // 2
LEVELS = 10
LAGS = (2, 4, 6, 8)


def encode(ref, value):
    lead = value.astype(jnp.bfloat16)
    wide = lead.astype(jnp.float32)
    safe = jnp.where(jnp.abs(wide) < 1e-36, 1.0, wide)
    steps = jnp.round((value - wide) * pl.reciprocal(safe, approx=True) * (256.0 * LEVELS))
    steps = jnp.clip(steps, -LEVELS, LEVELS)
    half = QN // 2
    ref[:, :QN] = lead
    ref[:, QN:] = (steps[:, :half] * (2 * LEVELS + 1) + steps[:, half:]).astype(jnp.bfloat16)


def decode(ref):
    wide = ref[:, :QN].astype(jnp.float32)
    code = ref[:, QN:].astype(jnp.float32)
    first = jnp.round(code * (1.0 / (2 * LEVELS + 1)))
    second = code - first * (2 * LEVELS + 1)
    return wide + wide * (jnp.concatenate([first, second], axis=1) * (1.0 / (256.0 * LEVELS)))


def kernel(
    tp_ref, amp_ref, int_hbm, lad_ref,
    g, wt, s_buf, t, fwd_out, fwd, rcv_out, rcv, zr, f, xr,
    int_sem, z_sem, x_sem, f_sem, t_sem, fwd_sem, rcv_sem, zr_sem, xr_sem,
):
    row, col = lax.axis_index("row"), lax.axis_index("col")
    x, zl, k = row // 4, (row // 2) % 2, row % 2
    zh, y = col // 4, col % 4

    def at_row(xx, zz, kk):
        return (xx * 4 + zz * 2 + kk, col)

    def at_col(cc):
        return (row, cc)

    xp, xm, xo = (x + 1) % 4, (x + 3) % 4, (x + 2) % 4
    yp, ym, yo = (y + 1) % 4, (y + 3) % 4, (y + 2) % 4
    right, left = at_row(xp, zl, k), at_row(xm, zl, k)
    zpart, twin = at_row(x, 1 - zl, k), at_row(x, zl, 1 - k)
    up, down = at_col(zh * 4 + yp), at_col(zh * 4 + ym)
    far = at_col((1 - zh) * 4 + y)

    loads = [pltpu.make_async_copy(int_hbm.at[e], wt.at[e], int_sem.at[e]) for e in range(5)]
    for c in loads:
        c.start()

    barrier = pltpu.get_barrier_semaphore()
    partners = [right, left, zpart, twin] + [at_col((col + d) % NB) for d in range(1, NB)]
    for p in partners:
        pl.semaphore_signal(barrier, inc=1, device_id=p, device_id_type=MESH)

    src = [tp_ref[e, 0] for e in range(5)]
    dst = [tp_ref[e, 1] for e in range(5)]
    counts = [sum((src[e] == v).astype(jnp.int32) for e in range(5)) for v in range(3)]
    lone = jnp.where(counts[0] == 1, 0, jnp.where(counts[1] == 1, 1, 2))
    first = jnp.where(lone == 0, 1, 0)
    second = jnp.where(lone == 2, 1, 2)

    def entry(a, b):
        found = jnp.int32(0)
        for e in range(1, 5):
            found = jnp.where((src[e] == a) & (dst[e] == b), e, found)
        return found

    e_l = entry(lone, lone)
    e_ff, e_sf = entry(first, first), entry(second, first)
    e_fs, e_ss = entry(first, second), entry(second, second)

    own = x * 2 + zl
    to = lax.broadcasted_iota(jnp.int32, (64, 64), 0)
    frm = lax.broadcasted_iota(jnp.int32, (64, 64), 1)
    block, mid, low = to // 8, (to // 2) % 2, to % 2
    distance = (block + NB - own) % NB
    direct = (distance < 4) | ((distance == 4) & (block >= 4))
    ilo, jlo = jnp.where(direct, mid, low), jnp.where(direct, low, mid)
    order64 = (frm == ilo * 32 + block * 4 + ((to // 4) % 2) * 2 + jlo).astype(jnp.bfloat16)
    for s, tile in ((2, second), (1, first), (0, lone)):
        g[s, own, k] = jnp.dot(order64, amp_ref[tile], preferred_element_type=jnp.float32).astype(jnp.bfloat16)
    pl.semaphore_wait(barrier, len(partners))

    def rdma(ref_src, ref_dst, ss, rs, dev):
        return pltpu.make_async_remote_copy(
            src_ref=ref_src, dst_ref=ref_dst, send_sem=ss, recv_sem=rs, device_id=dev, device_id_type=MESH
        )

    def chip(xx, zz):
        return xx * 2 + zz

    def cz(s, a, i=0):
        return rdma(g.at[s, a, k], g.at[s, a, k], z_sem.at[0, s, i], z_sem.at[1, s, i], zpart)

    def cx(s, a, side, which):
        return rdma(
            g.at[s, a, k], g.at[s, a, k], x_sem.at[0, s, side, which], x_sem.at[1, s, side, which],
            right if side == 0 else left,
        )

    def cf(s, a, side, which):
        part = g.at[s, a, k, pl.ds(32 * side, 32)]
        return rdma(part, part, f_sem.at[0, s, side, which], f_sem.at[1, s, side, which], right if side == 0 else left)

    def ct(s, a, i, kk=None):
        kk = k if kk is None else kk
        return rdma(g.at[s, a, kk], g.at[s, a, kk], t_sem.at[0, s, i], t_sem.at[1, s, i], twin)

    own_z = chip(x, 1 - zl)
    lefts, rights = (chip(xm, zl), chip(xm, 1 - zl)), (chip(xp, zl), chip(xp, 1 - zl))
    fars = (chip(xo, zl), chip(xo, 1 - zl))
    order = (own, own_z, *lefts, *rights, *fars)

    def send_own_z(s):
        cz(s, own).start()

    def send_own_x(s):
        cx(s, own, 0, 0).start()
        cx(s, own, 1, 0).start()
        ct(s, own, 0).start()

    def pass_z(s):
        cz(s, own_z).wait_recv()
        cx(s, own_z, 0, 1).start()
        cx(s, own_z, 1, 1).start()
        ct(s, own_z, 1).start()

    def pass_x(s, which):
        cx(s, lefts[which], 0, which).wait_recv()
        cf(s, lefts[which], 0, which).start()
        ct(s, lefts[which], 2 + which).start()
        cx(s, rights[which], 1, which).wait_recv()
        cf(s, rights[which], 1, which).start()
        ct(s, rights[which], 4 + which).start()

    def pass_far(s):
        for which in range(2):
            cf(s, fars[which], 0, which).wait_recv()
            cf(s, fars[which], 1, which).wait_recv()
            ct(s, fars[which], 6 + which).start()

    def end_twin(s):
        for i, a in enumerate(order):
            ct(s, a, i, 1 - k).wait_recv()

    def straight(s):
        cx(s, own, 0, 0).start()
        cx(s, own, 1, 0).start()
        ct(s, own, 0).start()

    def straight_pass(s):
        cx(s, lefts[0], 0, 0).wait_recv()
        cf(s, lefts[0], 0, 0).start()
        cx(s, rights[0], 1, 0).wait_recv()
        cf(s, rights[0], 1, 0).start()
        cz(s, lefts[0], 1).start()
        cz(s, rights[0], 2).start()
        ct(s, lefts[0], 2).start()
        ct(s, rights[0], 4).start()

    def straight_far(s):
        cf(s, fars[0], 0, 0).wait_recv()
        cf(s, fars[0], 1, 0).wait_recv()
        cz(s, fars[0], 3).start()
        ct(s, fars[0], 6).start()

    def straight_across(s, i, a, twin_at):
        cz(s, a, i).wait_recv()
        ct(s, a, twin_at).start()

    def end_sends(s):
        cz(s, own).wait_send()
        for side in range(2):
            cx(s, own, side, 0).wait_send()
            for which in range(1 if s == 2 else 2):
                cf(s, (lefts, rights)[side][which], side, which).wait_send()
            if s == 2:
                cz(s, (lefts, rights)[side][0], 1 + side).wait_send()
            else:
                cx(s, own_z, side, 1).wait_send()
        if s == 2:
            cz(s, fars[0], 3).wait_send()
        for i, a in enumerate(order):
            ct(s, a, i).wait_send()

    def c_fwd(r, side):
        rows = pl.ds(HALF * side, HALF - 16 * side)
        return rdma(
            fwd_out.at[r, rows], fwd.at[r, rows],
            fwd_sem.at[0, r, side], fwd_sem.at[1, r, side], up if side == 0 else down,
        )

    def c_rcv(r, side):
        return rdma(
            rcv_out.at[r, side], rcv.at[r, side],
            rcv_sem.at[0, r, side], rcv_sem.at[1, r, side], up if side == 0 else down,
        )

    def c_zr(r):
        start = pl.multiple_of(64 * (1 - zh), 8)
        return rdma(t.at[r, 2, pl.ds(start, 80)], zr.at[r], zr_sem.at[0, r], zr_sem.at[1, r], far)

    def c_xr(r, d):
        return rdma(f.at[r, d], xr.at[r, d - 1], xr_sem.at[0, r, d - 1], xr_sem.at[1, r, d - 1], at_col((col + d) % NB))

    def make_block(c, d):
        b = (c + d) % NB
        direct = s_buf[c, :, b]
        if d == 0:
            return direct
        other = s_buf[b, :, c]
        mirrored = jnp.stack(
            [
                jnp.concatenate([other[0, :4], other[1, :4]], axis=0),
                jnp.concatenate([other[0, 4:], other[1, 4:]], axis=0),
            ]
        )
        return direct + mirrored

    def stage1(r, pairs):
        n = r % RN
        columns = pl.ds(pl.multiple_of(n * QN, QN), QN)
        for m in range(4):
            total = None
            for slot, e in pairs:
                lhs = g[slot, 2 * m : 2 * m + 2].reshape(256, 2048)
                part = jnp.dot(lhs, wt[e, :, columns], preferred_element_type=jnp.float32)
                total = part if total is None else total + part
            s_buf[2 * m : 2 * m + 2] = total.reshape(2, 2, 8, 8, QN)
        for rel, yy in enumerate((yo, yp, ym, y)):
            at = 0
            for zz in range(2):
                for d in range(5 - zz):
                    rows = make_block(zz * 4 + yy, d).reshape(16, QN)
                    if rel == 0:
                        encode(fwd_out.at[r, pl.ds(at, 16)], rows)
                    else:
                        t[r, rel - 1, pl.ds(at, 16)] = rows
                    at += 16
            if rel == 0:
                c_fwd(r, 0).start()
                c_fwd(r, 1).start()

    def stage2(r):
        for side in range(2):
            c_fwd(r, side).wait_recv()
            for at in range(0, SET, 16):
                rows = pl.ds(at, 16)
                value = t[r, side, rows]
                if (at >= HALF) == (side == 1):
                    value = value + decode(fwd.at[r, rows])
                encode(rcv_out.at[r, side, rows], value)
            c_rcv(r, side).start()

    def stage3(r):
        c_rcv(r, 0).wait_recv()
        c_rcv(r, 1).wait_recv()
        for at in range(0, SET, 16):
            rows = pl.ds(at, 16)
            t[r, 2, rows] = t[r, 2, rows] + decode(rcv.at[r, 0, rows]) + decode(rcv.at[r, 1, rows])
        c_zr(r).start()

    def stage4(r):
        c_zr(r).wait_recv()
        mine = pl.ds(pl.multiple_of(80 * zh, 8), 64)
        theirs = pl.ds(pl.multiple_of(16 * zh, 8), 64)
        f[r, 0:4] = (t[r, 2, mine] + zr[r, theirs]).reshape(4, 16, QN)
        f[r, 4] = t[r, 2, pl.ds(64, 16)] + zr[r, pl.ds(64, 16)]
        for d in range(1, 4):
            c_xr(r, d).start()

        @pl.when(zh == 0)
        def _():
            c_xr(r, 4).start()

    def stage5(r):
        for d in range(1, 4):
            c_xr(r, d).wait_recv()

        @pl.when(zh == 1)
        def _():
            c_xr(r, 4).wait_recv()

        s, n = (r // RN + 1) % 3, r % RN
        columns = pl.ds(pl.multiple_of(n * QN, QN), QN)

        def place(block, b, swap):
            for i in range(4):
                for j in range(4):
                    p, q = (j, i) if swap else (i, j)
                    at = (p // 2) * 8 + (q // 2) * 4 + (p % 2) * 2 + q % 2
                    lad_ref[s, pl.ds(i * 32 + b * 4 + j, 1), columns] = block(at)

        def from_f(d):
            return lambda at: f[r, d, pl.ds(at, 1)]

        def from_xr(d):
            return lambda at: xr[r, d - 1, pl.ds(at, 1)]

        def at_of(p, q):
            return (p // 2) * 8 + (q // 2) * 4 + (p % 2) * 2 + q % 2

        for i in range(4):
            for j in range(4):
                lad_ref[s, pl.ds(i * 32 + col * 4 + j, 1), columns] = (
                    f[r, 0, pl.ds(at_of(i, j), 1)] + f[r, 0, pl.ds(at_of(j, i), 1)]
                )
        for d in range(1, 4):
            place(from_f(d), (col + d) % NB, False)
            place(from_xr(d), (col + NB - d) % NB, True)

        @pl.when(zh == 0)
        def _():
            place(from_f(4), (col + 4) % NB, False)

        @pl.when(zh == 1)
        def _():
            place(from_xr(4), (col + 4) % NB, True)

    send_own_z(1)
    straight(2)
    send_own_x(1)
    cz(2, own).start()
    pass_z(1)
    straight_pass(2)
    pass_x(1, 0)
    straight_across(2, 0, own_z, 1)
    straight_far(2)
    send_own_z(0)
    pass_x(1, 1)
    send_own_x(0)
    straight_across(2, 1, lefts[1], 3)
    straight_across(2, 2, rights[1], 5)
    pass_far(1)
    straight_across(2, 3, fars[1], 7)
    for c in loads:
        c.wait()
    end_twin(1)
    end_twin(2)
    pass_z(0)

    def step(it, carry):
        for when, hook in ((1, lambda: pass_x(0, 0)), (2, lambda: pass_x(0, 1)), (4, lambda: pass_far(0)), (8, lambda: end_twin(0))):
            pl.when(it == when)(hook)

        @pl.when(it < 2 * RN)
        def _():
            one = it < RN
            stage1(it, [(1, jnp.where(one, e_ff, e_fs)), (2, jnp.where(one, e_sf, e_ss))])

        @pl.when((it >= 2 * RN) & (it < ROUNDS))
        def _():
            stage1(it, [(0, e_l)])

        for lag, stage in zip(LAGS, (stage2, stage3, stage4, stage5)):
            @pl.when((it >= lag) & (it < ROUNDS + lag))
            def _(lag=lag, stage=stage):
                stage(it - lag)

        return carry

    lax.fori_loop(0, ROUNDS + LAGS[-1], step, 0)

    for s in range(3):
        end_sends(s)

    def drain(r, carry):
        for side in range(2):
            c_fwd(r, side).wait_send()
            c_rcv(r, side).wait_send()
        c_zr(r).wait_send()
        for d in range(1, 4):
            c_xr(r, d).wait_send()

        @pl.when(zh == 0)
        def _():
            c_xr(r, 4).wait_send()

        return carry

    lax.fori_loop(0, ROUNDS, drain, 0)


def ladder_call(tile_pairs, amplitudes, integrals):
    dma = pltpu.SemaphoreType.DMA
    return pl.pallas_call(
        kernel,
        out_shape=jax.ShapeDtypeStruct((3, 128, 1024), jnp.float32),
        in_specs=[
            pl.BlockSpec(memory_space=pltpu.SMEM),
            pl.BlockSpec(memory_space=pltpu.VMEM),
            pl.BlockSpec(memory_space=pl.ANY),
        ],
        out_specs=pl.BlockSpec(memory_space=pltpu.VMEM),
        scratch_shapes=[
            pltpu.VMEM((3, NB, 2, 64, 2048), jnp.bfloat16),
            pltpu.VMEM((5, 2048, 1024), jnp.bfloat16),
            pltpu.VMEM((NB, 2, NB, 8, QN), jnp.float32),
            pltpu.VMEM((ROUNDS, 3, SET, QN), jnp.float32),
            pltpu.VMEM((ROUNDS, SET, WIDE), jnp.bfloat16),
            pltpu.VMEM((ROUNDS, SET, WIDE), jnp.bfloat16),
            pltpu.VMEM((ROUNDS, 2, SET, WIDE), jnp.bfloat16),
            pltpu.VMEM((ROUNDS, 2, SET, WIDE), jnp.bfloat16),
            pltpu.VMEM((ROUNDS, 80, QN), jnp.float32),
            pltpu.VMEM((ROUNDS, 5, 16, QN), jnp.float32),
            pltpu.VMEM((ROUNDS, 4, 16, QN), jnp.float32),
            dma((5,)),
            dma((2, 3, 4)),
            dma((2, 3, 2, 2)),
            dma((2, 3, 2, 2)),
            dma((2, 3, 8)),
            dma((2, ROUNDS, 2)),
            dma((2, ROUNDS, 2)),
            dma((2, ROUNDS)),
            dma((2, ROUNDS, 4)),
        ],
        compiler_params=pltpu.CompilerParams(
            collective_id=0, has_side_effects=True, vmem_limit_bytes=60 << 20
        ),
        cost_estimate=pl.CostEstimate(flops=21_474_836_480, bytes_accessed=24 << 20, transcendentals=0),
    )(tile_pairs, amplitudes, integrals)


def lone_tile(tp_ref):
    counts = [sum((tp_ref[e, 0] == v).astype(jnp.int32) for e in range(5)) for v in range(3)]
    return jnp.where(counts[0] == 1, 0, jnp.where(counts[1] == 1, 1, 2))


def slot_of(tile, tp_ref):
    lone = lone_tile(tp_ref)
    return jnp.where(tile == lone, 0, 1 + tile - (tile > lone).astype(jnp.int32))


def finish(tp_ref, lad_ref, drv_ref, occ_ref, lead_ref, virt_ref, res_ref, upd_ref):
    row, col = lax.axis_index("row"), lax.axis_index("col")
    tile = pl.program_id(0)
    place = lax.broadcasted_iota(jnp.int32, (32, 128), 0)
    second = jnp.zeros((32, 128), jnp.float32)
    for j in range(32):
        second = jnp.where(place == j, occ_ref[j], second)
    inner = virt_ref[tile, 1:2, :]
    for c in range(8):
        columns = pl.ds(c * 128, 128)
        virtual_pair = lead_ref[tile, 0, row * 8 + c] + inner
        for i in range(4):
            rows = pl.ds(i * 32, 32)
            denominator = (occ_ref[col * 4 + i] + second) - virtual_pair
            residual = drv_ref[0, rows, columns].astype(jnp.float32) + lad_ref[0, rows, columns]
            res_ref[0, rows, columns] = residual
            upd_ref[0, rows, columns] = residual / denominator


def body(amplitudes, integrals, tile_pairs, driving, occupied_energy, virtual_energy):
    by_slot = ladder_call(tile_pairs, amplitudes, integrals)
    block = (1, 128, 1024)
    smem = pl.BlockSpec(memory_space=pltpu.SMEM)
    return pl.pallas_call(
        finish,
        out_shape=[jax.ShapeDtypeStruct(driving.shape, jnp.float32)] * 2,
        grid_spec=pltpu.PrefetchScalarGridSpec(
            num_scalar_prefetch=1,
            grid=(3,),
            in_specs=[
                pl.BlockSpec(block, lambda t, tp: (slot_of(t, tp), 0, 0)),
                pl.BlockSpec(block, lambda t, tp: (t, 0, 0)),
                smem,
                smem,
                pl.BlockSpec(virtual_energy.shape, lambda t, tp: (0, 0, 0)),
            ],
            out_specs=[pl.BlockSpec(block, lambda t, tp: (t, 0, 0))] * 2,
        ),
    )(tile_pairs, by_slot, driving, occupied_energy, virtual_energy, virtual_energy)


def solution(mesh):
    return jax.shard_map(
        body,
        mesh=mesh,
        in_specs=(
            P(None, "row", "col"),
            P(None, "col", "row"),
            P(),
            P(None, "col", "row"),
            P(),
            P(),
        ),
        out_specs=(P(None, "col", "row"), P(None, "col", "row")),
        check_vma=False,
    )
```

```python
import functools

import jax
import jax.numpy as jnp
from jax import lax
from jax.experimental import pallas as pl
from jax.experimental.pallas import tpu as pltpu
from jax.sharding import PartitionSpec as P

MESH = pl.DeviceIdType.MESH
NB = 8
QN = 256
RN = 4
ROUNDS = 12
SET = 144
HALF = 80
WIDE = QN + QN // 2
LEVELS = 10
LONE_LAGS, LAGS, Z_LAGS = (2, 4, 9, 13), (1, 3, 5, 10), (3, 4, 6, 10)
ZROUNDS = 3
GAP = 4


def encode(ref, value):
    lead = value.astype(jnp.bfloat16)
    wide = lead.astype(jnp.float32)
    safe = jnp.where(jnp.abs(wide) < 1e-36, 1.0, wide)
    steps = jnp.round((value - wide) * pl.reciprocal(safe, approx=True) * (256.0 * LEVELS))
    steps = jnp.clip(steps, -LEVELS, LEVELS)
    half = QN // 2
    ref[:, :QN] = lead
    ref[:, QN:] = (steps[:, :half] * (2 * LEVELS + 1) + steps[:, half:]).astype(jnp.bfloat16)


def decode(ref):
    wide = ref[:, :QN].astype(jnp.float32)
    code = ref[:, QN:].astype(jnp.float32)
    first = jnp.round(code * (1.0 / (2 * LEVELS + 1)))
    second = code - first * (2 * LEVELS + 1)
    return wide + wide * (jnp.concatenate([first, second], axis=1) * (1.0 / (256.0 * LEVELS)))


def kernel(
    tp_ref, amp_ref, int_hbm, out_ref,
    g, wt, s_buf, t, t_far, fwd_out, fwd, rcv_out, rcv, zf_out, zf, zr_out, zr, f, xr_out, xr, lad_ref,
    int_sem, z_sem, x_sem, f_sem, t_sem, fwd_sem, rcv_sem, zr_sem, xr_sem, send_sem,
):
    row, col = lax.axis_index("row"), lax.axis_index("col")
    x, zl, k = row // 4, (row // 2) % 2, row % 2
    zh, y = col // 4, col % 4

    def at_row(xx, zz, kk):
        return (xx * 4 + zz * 2 + kk, col)

    def at_col(cc):
        return (row, cc)

    xp, xm, xo = (x + 1) % 4, (x + 3) % 4, (x + 2) % 4
    yp, ym, yo = (y + 1) % 4, (y + 3) % 4, (y + 2) % 4
    right, left = at_row(xp, zl, k), at_row(xm, zl, k)
    zpart, twin = at_row(x, 1 - zl, k), at_row(x, zl, 1 - k)
    up, down = at_col(zh * 4 + yp), at_col(zh * 4 + ym)
    far = at_col((1 - zh) * 4 + y)

    load = pltpu.make_async_copy(int_hbm, wt, int_sem)
    load.start()

    barrier = pltpu.get_barrier_semaphore()
    partners = [right, left, zpart, twin] + [at_col((col + d) % NB) for d in range(1, NB)]
    for p in partners:
        pl.semaphore_signal(barrier, inc=1, device_id=p, device_id_type=MESH)

    pairs = tp_ref[...]
    src = [pairs[0, e] for e in range(5)]
    dst = [pairs[1, e] for e in range(5)]
    counts = [sum((src[e] == v).astype(jnp.int32) for e in range(5)) for v in range(3)]
    lone = jnp.where(counts[0] == 1, 0, jnp.where(counts[1] == 1, 1, 2))
    first = jnp.where(lone == 0, 1, 0)
    second = jnp.where(lone == 2, 1, 2)

    def entry(a, b):
        found = jnp.int32(0)
        for e in range(1, 5):
            found = jnp.where((src[e] == a) & (dst[e] == b), e, found)
        return found

    e_l = entry(lone, lone)
    e_ff, e_sf = entry(first, first), entry(second, first)
    e_fs, e_ss = entry(first, second), entry(second, second)

    own = x * 2 + zl
    to = lax.broadcasted_iota(jnp.int32, (64, 64), 0)
    frm = lax.broadcasted_iota(jnp.int32, (64, 64), 1)
    block, mid, low = to // 8, (to // 2) % 2, to % 2
    distance = (block + NB - own) % NB
    direct = (distance < 4) | ((distance == 4) & (block >= 4))
    ilo, jlo = jnp.where(direct, mid, low), jnp.where(direct, low, mid)
    order64 = (frm == ilo * 32 + block * 4 + ((to // 4) % 2) * 2 + jlo).astype(jnp.bfloat16)
    for s, tile in ((0, lone), (2, second), (1, first)):
        g[s, own, k] = jnp.dot(order64, amp_ref[tile], preferred_element_type=jnp.float32).astype(jnp.bfloat16)
    pl.semaphore_wait(barrier, len(partners))

    def rdma(ref_src, ref_dst, ss, rs, dev):
        return pltpu.make_async_remote_copy(
            src_ref=ref_src, dst_ref=ref_dst, send_sem=ss, recv_sem=rs, device_id=dev, device_id_type=MESH
        )

    def chip(xx, zz):
        return xx * 2 + zz

    def cz(s, a, i=0):
        return rdma(g.at[s, a, k], g.at[s, a, k], send_sem.at[0], z_sem.at[s + i], zpart)

    def cx(s, a, side, which):
        return rdma(g.at[s, a, k], g.at[s, a, k], send_sem.at[1], x_sem.at[s, side, which], right if side == 0 else left)

    def cf(s, a, side, which):
        part = g.at[s, a, k, pl.ds(32 * side, 32)]
        return rdma(part, part, send_sem.at[2], f_sem.at[s, which], right if side == 0 else left)

    def far_arrived(s, which):
        whole = g.at[s, fars[which], k]
        rdma(whole, whole, send_sem.at[2], f_sem.at[s, which], right).wait_recv()

    def ct(s, a):
        return rdma(g.at[s, a, k], g.at[s, a, k], send_sem.at[3], t_sem.at[s], twin)

    own_z = chip(x, 1 - zl)
    lefts, rights = (chip(xm, zl), chip(xm, 1 - zl)), (chip(xp, zl), chip(xp, 1 - zl))
    fars = (chip(xo, zl), chip(xo, 1 - zl))

    def send_own_z(s):
        cz(s, own).start()

    def send_own_x(s):
        cx(s, own, 0, 0).start()
        cx(s, own, 1, 0).start()
        ct(s, own).start()

    def pass_z(s):
        cz(s, own_z).wait_recv()
        cx(s, own_z, 0, 1).start()
        cx(s, own_z, 1, 1).start()
        ct(s, own_z).start()

    def pass_x(s, which):
        cx(s, lefts[which], 0, which).wait_recv()
        cf(s, lefts[which], 0, which).start()
        ct(s, lefts[which]).start()
        cx(s, rights[which], 1, which).wait_recv()
        cf(s, rights[which], 1, which).start()
        ct(s, rights[which]).start()

    def pass_far(s):
        for which in range(2):
            far_arrived(s, which)
            ct(s, fars[which]).start()

    def end_twin(s):
        half = g.at[s, :, 1 - k]
        rdma(half, half, send_sem.at[3], t_sem.at[s], twin).wait_recv()

    def straight(s):
        cx(s, own, 0, 0).start()
        cx(s, own, 1, 0).start()
        ct(s, own).start()

    def straight_pass(s):
        cx(s, lefts[0], 0, 0).wait_recv()
        cf(s, lefts[0], 0, 0).start()
        cx(s, rights[0], 1, 0).wait_recv()
        cf(s, rights[0], 1, 0).start()
        cz(s, lefts[0], 1).start()
        cz(s, rights[0], 2).start()
        ct(s, lefts[0]).start()
        ct(s, rights[0]).start()

    def straight_far(s):
        far_arrived(s, 0)
        cz(s, fars[0], 3).start()
        ct(s, fars[0]).start()

    def straight_across(s, i, a):
        cz(s, a, i).wait_recv()
        ct(s, a).start()

    def sent(ref, i):
        rdma(ref, ref, send_sem.at[i], z_sem.at[0], twin).wait_send()

    def end_sends():
        sent(g.at[0, 0:3], 0)
        sent(g.at[0, 0:5], 1)
        sent(g.at[0, 0:5, 0], 2)
        sent(g.at[:, :, 0], 3)
        sent(fwd_out.at[0 : ROUNDS - ZROUNDS], 4)
        sent(fwd_out.at[0:ZROUNDS, pl.ds(0, HALF)], 5)
        sent(rcv_out.at[0 : ROUNDS - ZROUNDS], 6)
        sent(rcv_out.at[0:ZROUNDS, :, pl.ds(0, HALF)], 7)
        sent(zr.at[0 : ROUNDS - ZROUNDS], 8)
        sent(zf_out, 9)

        @pl.when(zh == 0)
        def _():
            sent(xr_out, 10)

        @pl.when(zh == 1)
        def _():
            sent(xr_out.at[:, 0:3], 10)

    def c_fwd(r, side, zfirst):
        top, low = (48, 32) if zfirst else (HALF, SET - HALF)
        rows = pl.ds(top * side, low if side else top)
        return rdma(
            fwd_out.at[r, rows], fwd.at[r, rows], send_sem.at[4 + zfirst], fwd_sem.at[r], up if side == 0 else down
        )

    def c_rcv(r, side, zfirst):
        rows = pl.ds(0, HALF if zfirst else SET)
        return rdma(
            rcv_out.at[r, side, rows], rcv.at[r, side, rows],
            send_sem.at[6 + zfirst], rcv_sem.at[r], up if side == 0 else down,
        )

    def arrived(ref, sem):
        rdma(ref, ref, send_sem.at[4], sem, twin).wait_recv()

    def c_zr(r):
        return rdma(zr_out.at[r], zr.at[r], send_sem.at[8], zr_sem.at[r], far)

    def c_zf(q, r):
        return rdma(zf_out.at[q], zf.at[q], send_sem.at[9], zr_sem.at[r], far)

    def c_xr(r, d):
        return rdma(xr_out.at[r, d - 1], xr.at[r, d - 1], send_sem.at[10], xr_sem.at[r], at_col((col + d) % NB))

    def zfirst_of(r):
        return (r >= RN) & (r < ROUNDS - 2) & (r % 2 == 0)

    def both(stage, zstage):
        def run(r):
            pl.when(jnp.logical_not(zfirst_of(r)))(lambda: stage(r))
            pl.when(zfirst_of(r))(lambda: zstage(r, (r - RN) // 2))

        return run

    def mine(at):
        return pl.ds(pl.multiple_of(64 * zh + at, 16), 16)

    def others(at):
        return pl.ds(pl.multiple_of(64 * (1 - zh) + at, 16), 16)

    def make_block(c, d):
        b = (c + d) % NB
        direct = s_buf[c, :, b]
        if d == 0:
            return direct
        other = s_buf[b, :, c]
        mirrored = jnp.stack(
            [
                jnp.concatenate([other[0, :4], other[1, :4]], axis=0),
                jnp.concatenate([other[0, 4:], other[1, 4:]], axis=0),
            ]
        )
        return direct + mirrored

    def stage1(r, pairs):
        n = r % RN
        columns = pl.ds(pl.multiple_of(n * QN, QN), QN)
        for m in range(4):
            total = None
            for slot, e in pairs:
                lhs = g[slot, 2 * m : 2 * m + 2].reshape(256, 2048)
                part = jnp.dot(lhs, wt[e, :, columns], preferred_element_type=jnp.float32)
                total = part if total is None else total + part
            s_buf[2 * m : 2 * m + 2] = total.reshape(2, 2, 8, 8, QN)
        def form(store):
            for rel, yy in enumerate((yo, yp, ym, y)):
                at = 0
                for zz in range(2):
                    for d in range(5 - zz):
                        store(rel, pl.ds(at, 16), make_block(zz * 4 + yy, d).reshape(16, QN))
                        at += 16

        def form_y(r):
            def store(rel, rows, value):
                if rel == 0:
                    encode(fwd_out.at[r, rows], value)
                else:
                    t[r, rel - 1, rows] = value

            form(store)
            c_fwd(r, 0, 0).start()
            c_fwd(r, 1, 0).start()

        def form_z(r, q):
            def store(rel, rows, value):
                if rel == 0:
                    t_far[q, rows] = value
                else:
                    t[r, rel - 1, rows] = value

            form(store)
            for at in range(0, HALF, 16):
                encode(zf_out.at[q, 0, pl.ds(at, 16)], t_far[q, others(at)])
                for rel in range(3):
                    encode(zf_out.at[q, 1 + rel, pl.ds(at, 16)], t[r, rel, others(at)])
            c_zf(q, r).start()

        if len(pairs) == 1:
            form_y(r)
        else:
            both(form_y, form_z)(r)

    def stage2_y(r):
        arrived(fwd.at[r], fwd_sem.at[r])
        for side in range(2):
            for at in range(0, SET, 16):
                rows = pl.ds(at, 16)
                value = t[r, side, rows]
                if (at >= HALF) == (side == 1):
                    value = value + decode(fwd.at[r, rows])
                encode(rcv_out.at[r, side, rows], value)
            c_rcv(r, side, 0).start()

    def stage2_z(r, q):
        arrived(zf.at[q], zr_sem.at[r])
        for at in range(0, HALF, 16):
            rows = pl.ds(at, 16)
            encode(fwd_out.at[r, rows], t_far[q, mine(at)] + decode(zf.at[q, 0, rows]))
        c_fwd(r, 0, 1).start()
        c_fwd(r, 1, 1).start()
        for rel in range(3):
            for at in range(0, HALF, 16):
                t[r, rel, mine(at)] = t[r, rel, mine(at)] + decode(zf.at[q, 1 + rel, pl.ds(at, 16)])

    def stage3_y(r):
        arrived(rcv.at[r], rcv_sem.at[r])
        for at in range(0, SET, 16):
            rows = pl.ds(at, 16)
            t[r, 2, rows] = t[r, 2, rows] + decode(rcv.at[r, 0, rows]) + decode(rcv.at[r, 1, rows])
        for at in range(0, HALF, 16):
            encode(zr_out.at[r, pl.ds(at, 16)], t[r, 2, others(at)])
        c_zr(r).start()

    def stage3_z(r, q):
        arrived(fwd.at[r, pl.ds(0, HALF)], fwd_sem.at[r])
        for side in range(2):
            for at in range(0, HALF, 16):
                rows = pl.ds(at, 16)
                value = t[r, side, mine(at)]
                if (at >= 48) == (side == 1):
                    value = value + decode(fwd.at[r, rows])
                encode(rcv_out.at[r, side, rows], value)
            c_rcv(r, side, 1).start()

    def exchange(r):
        for d in range(1, 5):
            encode(xr_out.at[r, d - 1], f[r, d])
            if d < 4:
                c_xr(r, d).start()

        @pl.when(zh == 0)
        def _():
            c_xr(r, 4).start()

    def stage4_y(r):
        arrived(zr.at[r], zr_sem.at[r])
        own_rows = pl.ds(pl.multiple_of(HALF * zh, 16), 64)
        theirs = pl.ds(pl.multiple_of(16 * zh, 16), 64)
        f[r, 0:4] = (t[r, 2, own_rows] + decode(zr.at[r, theirs])).reshape(4, 16, QN)
        f[r, 4] = t[r, 2, pl.ds(64, 16)] + decode(zr.at[r, pl.ds(64, 16)])
        exchange(r)

    def stage4_z(r, q):
        arrived(rcv.at[r, :, pl.ds(0, HALF)], rcv_sem.at[r])
        for at in range(0, HALF, 16):
            rows = pl.ds(at, 16)
            t[r, 2, rows] = t[r, 2, mine(at)] + decode(rcv.at[r, 0, rows]) + decode(rcv.at[r, 1, rows])
        f[r, 0:4] = t[r, 2, pl.ds(pl.multiple_of(16 * zh, 16), 64)].reshape(4, 16, QN)
        f[r, 4] = t[r, 2, pl.ds(64, 16)]
        exchange(r)

    def stage5(r):
        @pl.when(zh == 0)
        def _():
            arrived(xr.at[r, 0:3], xr_sem.at[r])

        @pl.when(zh == 1)
        def _():
            arrived(xr.at[r], xr_sem.at[r])

        s, n = r // RN, r % RN
        columns = pl.ds(pl.multiple_of(n * QN, QN), QN)

        def place(block, b, swap):
            for i in range(4):
                for j in range(4):
                    p, q = (j, i) if swap else (i, j)
                    at = (p // 2) * 8 + (q // 2) * 4 + (p % 2) * 2 + q % 2
                    lad_ref[s, pl.ds(i * 32 + b * 4 + j, 1), columns] = block(at)

        def from_f(d):
            return lambda at: f[r, d, pl.ds(at, 1)]

        def from_xr(d):
            value = decode(xr.at[r, d - 1])
            return lambda at: value[at : at + 1]

        def at_of(p, q):
            return (p // 2) * 8 + (q // 2) * 4 + (p % 2) * 2 + q % 2

        for i in range(4):
            for j in range(4):
                lad_ref[s, pl.ds(i * 32 + col * 4 + j, 1), columns] = (
                    f[r, 0, pl.ds(at_of(i, j), 1)] + f[r, 0, pl.ds(at_of(j, i), 1)]
                )
        for d in range(1, 4):
            place(from_f(d), (col + d) % NB, False)
            place(from_xr(d), (col + NB - d) % NB, True)

        @pl.when(zh == 0)
        def _():
            place(from_f(4), (col + 4) % NB, False)

        @pl.when(zh == 1)
        def _():
            place(from_xr(4), (col + 4) % NB, True)

    stages = ((stage2_y, stage2_z), (stage3_y, stage3_z), (stage4_y, stage4_z), (stage5, None))

    send_own_z(0)
    send_own_x(0)
    pass_z(0)
    cz(2, own).start()
    send_own_z(1)
    pass_x(0, 0)
    pass_x(0, 1)
    straight(2)
    send_own_x(1)
    pass_far(0)
    load.wait()
    end_twin(0)

    def gather1():
        straight_across(2, 0, own_z)
        straight_pass(2)
        pass_z(1)

    def gather3():
        pass_x(1, 0)

    def gather4():
        straight_far(2)

    def gather6():
        straight_across(2, 1, lefts[1])
        pass_x(1, 1)
        straight_across(2, 2, rights[1])

    def gather8():
        pass_far(1)
        straight_across(2, 3, fars[1])
        end_twin(1)
        end_twin(2)

    def step(it, carry):
        for when, hook in ((1, gather1), (3, gather3), (4, gather4), (6, gather6), (8, gather8)):
            pl.when(it == when)(hook)

        @pl.when(it < RN)
        def _():
            stage1(it, [(0, e_l)])

        @pl.when((it >= RN + GAP) & (it < ROUNDS + GAP))
        def _():
            one = it < 2 * RN + GAP
            stage1(it - GAP, [(1, jnp.where(one, e_ff, e_fs)), (2, jnp.where(one, e_sf, e_ss))])

        for n in range(4):
            stage, zstage = stages[n]
            lone_r, r, z_r = it - LONE_LAGS[n], it - GAP - LAGS[n], it - GAP - Z_LAGS[n]
            is_lone = (lone_r >= 0) & (lone_r < RN)
            is_pair = (r >= RN) & (r < ROUNDS)
            if zstage is None:
                pl.when(is_lone)(lambda: stage(lone_r))
                pl.when(is_pair)(lambda: stage(r))
            else:
                pl.when(is_lone)(lambda: stage(lone_r))
                pl.when(is_pair & jnp.logical_not(zfirst_of(r)))(lambda: stage(r))
                pl.when(zfirst_of(z_r))(lambda: zstage(z_r, (z_r - RN) // 2))

        return carry

    lax.fori_loop(0, ROUNDS + GAP + LAGS[-1], step, 0)

    for tile in range(3):
        out_ref[tile] = lad_ref[jnp.where(lone == tile, 0, 1 + tile - jnp.where(lone < tile, 1, 0))]
    end_sends()


def ladder_call(tile_pairs, amplitudes, integrals):
    dma = pltpu.SemaphoreType.DMA
    return pl.pallas_call(
        kernel,
        out_shape=jax.ShapeDtypeStruct((3, 128, 1024), jnp.float32),
        in_specs=[
            pl.BlockSpec(memory_space=pltpu.VMEM),
            pl.BlockSpec(memory_space=pltpu.VMEM),
            pl.BlockSpec(memory_space=pl.ANY),
        ],
        out_specs=pl.BlockSpec(memory_space=pltpu.VMEM),
        scratch_shapes=[
            pltpu.VMEM((3, NB, 2, 64, 2048), jnp.bfloat16),
            pltpu.VMEM((5, 2048, 1024), jnp.bfloat16),
            pltpu.VMEM((NB, 2, NB, 8, QN), jnp.float32),
            pltpu.VMEM((ROUNDS, 3, SET, QN), jnp.float32),
            pltpu.VMEM((ZROUNDS, SET, QN), jnp.float32),
            pltpu.VMEM((ROUNDS, SET, WIDE), jnp.bfloat16),
            pltpu.VMEM((ROUNDS, SET, WIDE), jnp.bfloat16),
            pltpu.VMEM((ROUNDS, 2, SET, WIDE), jnp.bfloat16),
            pltpu.VMEM((ROUNDS, 2, SET, WIDE), jnp.bfloat16),
            pltpu.VMEM((ZROUNDS, 4, HALF, WIDE), jnp.bfloat16),
            pltpu.VMEM((ZROUNDS, 4, HALF, WIDE), jnp.bfloat16),
            pltpu.VMEM((ROUNDS, HALF, WIDE), jnp.bfloat16),
            pltpu.VMEM((ROUNDS, HALF, WIDE), jnp.bfloat16),
            pltpu.VMEM((ROUNDS, 5, 16, QN), jnp.float32),
            pltpu.VMEM((ROUNDS, 4, 16, WIDE), jnp.bfloat16),
            pltpu.VMEM((ROUNDS, 4, 16, WIDE), jnp.bfloat16),
            pltpu.VMEM((3, 128, 1024), jnp.float32),
            dma,
            dma((6,)),
            dma((3, 2, 2)),
            dma((3, 2)),
            dma((3,)),
            dma((ROUNDS,)),
            dma((ROUNDS,)),
            dma((ROUNDS,)),
            dma((ROUNDS,)),
            dma((11,)),
        ],
        compiler_params=pltpu.CompilerParams(
            collective_id=0, has_side_effects=True, vmem_limit_bytes=60 << 20
        ),
        cost_estimate=pl.CostEstimate(flops=21_474_836_480, bytes_accessed=24 << 20, transcendentals=0),
    )(tile_pairs, amplitudes, integrals)


def finish(lad_hbm, drv_hbm, occ_ref, virt_ref, res_hbm, upd_hbm, lad_ref, drv_ref, res_ref, upd_ref, sem):
    row, col = lax.axis_index("row"), lax.axis_index("col")
    reads = []
    for tile in range(3):
        reads.append(pltpu.make_async_copy(lad_hbm.at[tile], lad_ref.at[tile], sem.at[0, tile]))
        reads.append(pltpu.make_async_copy(drv_hbm.at[tile], drv_ref.at[tile], sem.at[1, tile]))
    for c in reads:
        c.start()
    lanes = occ_ref[...].reshape(1, 32)
    across = lax.broadcasted_iota(jnp.int32, (32, 32), 1)
    eye = lax.broadcasted_iota(jnp.int32, (32, 32), 0) == across
    second = jnp.sum(jnp.where(eye, jnp.broadcast_to(lanes, (32, 32)), 0.0), axis=1, keepdims=True)
    place = lax.broadcasted_iota(jnp.int32, (1, 128), 1)
    sums = []
    for i in range(4):
        here = jnp.sum(jnp.where(across[:1] == col * 4 + i, lanes, 0.0), axis=1, keepdims=True)
        sums.append(jnp.broadcast_to(here + second, (32, 128)))
    writes = []
    for tile in range(3):
        inner, outer = virt_ref[tile, 1:2, :], virt_ref[tile, 0:1, :]
        reads[2 * tile].wait()
        reads[2 * tile + 1].wait()
        for c in range(8):
            columns = pl.ds(c * 128, 128)
            lead = jnp.sum(jnp.where(place == row * 8 + c, outer, 0.0), axis=1, keepdims=True)
            virtual_pair = lead + inner
            for i in range(4):
                rows = pl.ds(i * 32, 32)
                residual = drv_ref[tile, rows, columns].astype(jnp.float32) + lad_ref[tile, rows, columns]
                res_ref[tile, rows, columns] = residual
                upd_ref[tile, rows, columns] = residual / (sums[i] - virtual_pair)
        writes.append(pltpu.make_async_copy(res_ref.at[tile], res_hbm.at[tile], sem.at[2, tile]))
        writes.append(pltpu.make_async_copy(upd_ref.at[tile], upd_hbm.at[tile], sem.at[3, tile]))
        writes[-2].start()
        writes[-1].start()
    for c in writes:
        c.wait()


def body(amplitudes, integrals, tile_pairs, driving, occupied_energy, virtual_energy):
    ladder = ladder_call(tile_pairs.T, amplitudes, integrals)
    vmem, anywhere = pl.BlockSpec(memory_space=pltpu.VMEM), pl.BlockSpec(memory_space=pl.ANY)
    out = jax.ShapeDtypeStruct(driving.shape, jnp.float32)
    held = pltpu.VMEM(driving.shape, jnp.float32)
    return pl.pallas_call(
        finish,
        out_shape=[out, out],
        in_specs=[anywhere, anywhere, vmem, vmem],
        out_specs=[anywhere, anywhere],
        scratch_shapes=[held, pltpu.VMEM(driving.shape, jnp.bfloat16), held, held, pltpu.SemaphoreType.DMA((4, 3))],
        compiler_params=pltpu.CompilerParams(vmem_limit_bytes=60 << 20),
    )(ladder, driving, occupied_energy, virtual_energy)


def solution(mesh):
    return jax.shard_map(
        body,
        mesh=mesh,
        in_specs=(
            P(None, "row", "col"),
            P(None, "col", "row"),
            P(),
            P(None, "col", "row"),
            P(),
            P(),
        ),
        out_specs=(P(None, "col", "row"), P(None, "col", "row")),
        check_vma=False,
    )
```

```python
import functools

import jax
import jax.numpy as jnp
from jax import lax
from jax.experimental import pallas as pl
from jax.experimental.pallas import tpu as pltpu
from jax.sharding import PartitionSpec as P

MESH = pl.DeviceIdType.MESH
NB = 8
QN = 256
RN = 4
ROUNDS = 12
SET = 144
HALF = 80
WIDE = QN + QN // 2
LEVELS = 10
LONE_LAGS, LAGS, Z_LAGS = (2, 7, 10, 14), (1, 3, 5, 10), (3, 4, 6, 10)
ZROUNDS = 2
GAP = 4


def encode(ref, value):
    lead = value.astype(jnp.bfloat16)
    wide = lead.astype(jnp.float32)
    safe = jnp.where(jnp.abs(wide) < 1e-36, 1.0, wide)
    steps = jnp.round((value - wide) * pl.reciprocal(safe, approx=True) * (256.0 * LEVELS))
    steps = jnp.clip(steps, -LEVELS, LEVELS)
    half = QN // 2
    ref[:, :QN] = lead
    ref[:, QN:] = (steps[:, :half] * (2 * LEVELS + 1) + steps[:, half:]).astype(jnp.bfloat16)


def decode(ref):
    wide = ref[:, :QN].astype(jnp.float32)
    code = ref[:, QN:].astype(jnp.float32)
    first = jnp.round(code * (1.0 / (2 * LEVELS + 1)))
    second = code - first * (2 * LEVELS + 1)
    return wide + wide * (jnp.concatenate([first, second], axis=1) * (1.0 / (256.0 * LEVELS)))


def read_pairs(tp_ref):
    pairs = tp_ref[...]
    src = [pairs[0, e] for e in range(5)]
    dst = [pairs[1, e] for e in range(5)]
    counts = [sum((src[e] == v).astype(jnp.int32) for e in range(5)) for v in range(3)]
    return src, dst, jnp.where(counts[0] == 1, 0, jnp.where(counts[1] == 1, 1, 2))


def kernel(
    tp_ref, amp_hbm, int_hbm, out_hbm,
    g, wt, s_buf, t, t_far, fwd_out, fwd, rcv_out, rcv, zf_out, zf, zr_out, zr, f, xr_out, xr, lad_ref, amp_ref,
    int_sem, z_sem, x_sem, f_sem, t_sem, fwd_sem, rcv_sem, zr_sem, xr_sem, send_sem, own_sem,
):
    row, col = lax.axis_index("row"), lax.axis_index("col")
    x, zl, k = row // 4, (row // 2) % 2, row % 2
    zh, y = col // 4, col % 4

    def at_row(xx, zz, kk):
        return (xx * 4 + zz * 2 + kk, col)

    def at_col(cc):
        return (row, cc)

    xp, xm, xo = (x + 1) % 4, (x + 3) % 4, (x + 2) % 4
    yp, ym, yo = (y + 1) % 4, (y + 3) % 4, (y + 2) % 4
    right, left = at_row(xp, zl, k), at_row(xm, zl, k)
    zpart, twin = at_row(x, 1 - zl, k), at_row(x, zl, 1 - k)
    up, down = at_col(zh * 4 + yp), at_col(zh * 4 + ym)
    far = at_col((1 - zh) * 4 + y)

    load_own = pltpu.make_async_copy(amp_hbm, amp_ref, own_sem.at[3])
    load_own.start()

    barrier = pltpu.get_barrier_semaphore()
    partners = [right, left, zpart, twin] + [at_col((col + d) % NB) for d in range(1, NB)]
    for p in partners:
        pl.semaphore_signal(barrier, inc=1, device_id=p, device_id_type=MESH)
    load = pltpu.make_async_copy(int_hbm, wt, int_sem)
    load.start()

    src, dst, lone = read_pairs(tp_ref)
    first = jnp.where(lone == 0, 1, 0)
    second = jnp.where(lone == 2, 1, 2)

    def entry(a, b):
        found = jnp.int32(0)
        for e in range(1, 5):
            found = jnp.where((src[e] == a) & (dst[e] == b), e, found)
        return found

    e_l = entry(lone, lone)
    e_ff, e_sf = entry(first, first), entry(second, first)
    e_fs, e_ss = entry(first, second), entry(second, second)

    own = x * 2 + zl
    to = lax.broadcasted_iota(jnp.int32, (64, 64), 0)
    frm = lax.broadcasted_iota(jnp.int32, (64, 64), 1)
    block, mid, low = to // 8, (to // 2) % 2, to % 2
    distance = (block + NB - own) % NB
    direct = (distance < 4) | ((distance == 4) & (block >= 4))
    ilo, jlo = jnp.where(direct, mid, low), jnp.where(direct, low, mid)
    order64 = (frm == ilo * 32 + block * 4 + ((to // 4) % 2) * 2 + jlo).astype(jnp.bfloat16)
    load_own.wait()
    for s, tile in ((0, lone), (2, second), (1, first)):
        g[s, own, k] = jnp.dot(order64, amp_ref[tile], preferred_element_type=jnp.float32).astype(jnp.bfloat16)
    pl.semaphore_wait(barrier, len(partners))

    def rdma(ref_src, ref_dst, ss, rs, dev):
        return pltpu.make_async_remote_copy(
            src_ref=ref_src, dst_ref=ref_dst, send_sem=ss, recv_sem=rs, device_id=dev, device_id_type=MESH
        )

    def chip(xx, zz):
        return xx * 2 + zz

    def cz(s, a, i=0):
        return rdma(g.at[s, a, k], g.at[s, a, k], send_sem.at[0], z_sem.at[s + i], zpart)

    def cx(s, a, side, which):
        return rdma(g.at[s, a, k], g.at[s, a, k], send_sem.at[1], x_sem.at[s, side, which], right if side == 0 else left)

    def cf(s, a, side, which):
        part = g.at[s, a, k, pl.ds(32 * side, 32)]
        return rdma(part, part, send_sem.at[2], f_sem.at[s, which], right if side == 0 else left)

    def far_arrived(s, which):
        whole = g.at[s, fars[which], k]
        rdma(whole, whole, send_sem.at[2], f_sem.at[s, which], right).wait_recv()

    def ct(s, a):
        return rdma(g.at[s, a, k], g.at[s, a, k], send_sem.at[3], t_sem.at[s], twin)

    own_z = chip(x, 1 - zl)
    lefts, rights = (chip(xm, zl), chip(xm, 1 - zl)), (chip(xp, zl), chip(xp, 1 - zl))
    fars = (chip(xo, zl), chip(xo, 1 - zl))

    def send_own_z(s):
        cz(s, own).start()

    def send_own_x(s):
        cx(s, own, 0, 0).start()
        cx(s, own, 1, 0).start()
        ct(s, own).start()

    def pass_z(s):
        cz(s, own_z).wait_recv()
        cx(s, own_z, 0, 1).start()
        cx(s, own_z, 1, 1).start()
        ct(s, own_z).start()

    def pass_x(s, which):
        cx(s, lefts[which], 0, which).wait_recv()
        cf(s, lefts[which], 0, which).start()
        ct(s, lefts[which]).start()
        cx(s, rights[which], 1, which).wait_recv()
        cf(s, rights[which], 1, which).start()
        ct(s, rights[which]).start()

    def pass_far(s):
        for which in range(2):
            far_arrived(s, which)
            ct(s, fars[which]).start()

    def end_twin(s):
        half = g.at[s, :, 1 - k]
        rdma(half, half, send_sem.at[3], t_sem.at[s], twin).wait_recv()

    def straight(s):
        cx(s, own, 0, 0).start()
        cx(s, own, 1, 0).start()
        ct(s, own).start()

    def straight_pass(s):
        cx(s, lefts[0], 0, 0).wait_recv()
        cf(s, lefts[0], 0, 0).start()
        cx(s, rights[0], 1, 0).wait_recv()
        cf(s, rights[0], 1, 0).start()
        cz(s, lefts[0], 1).start()
        cz(s, rights[0], 2).start()
        ct(s, lefts[0]).start()
        ct(s, rights[0]).start()

    def straight_far(s):
        far_arrived(s, 0)
        cz(s, fars[0], 3).start()
        ct(s, fars[0]).start()

    def straight_across(s, i, a):
        cz(s, a, i).wait_recv()
        ct(s, a).start()

    def sent(ref, i):
        rdma(ref, ref, send_sem.at[i], z_sem.at[0], twin).wait_send()

    def end_sends():
        sent(g.at[0, 0:7, 0], 0)
        sent(g.at[0, 0:5], 1)
        sent(g.at[0, 0:2], 2)
        sent(g.at[:, :, 0], 3)
        sent(fwd_out.at[0 : ROUNDS - ZROUNDS], 4)
        sent(fwd_out.at[0:ZROUNDS, pl.ds(0, HALF)], 5)
        sent(rcv_out.at[0 : ROUNDS - ZROUNDS], 6)
        sent(rcv_out.at[0:ZROUNDS, :, pl.ds(0, HALF)], 7)
        sent(zr.at[0 : ROUNDS - ZROUNDS], 8)
        sent(zf_out, 9)

        @pl.when(zh == 0)
        def _():
            sent(xr_out, 10)

        @pl.when(zh == 1)
        def _():
            sent(xr_out.at[:, 0:3], 10)

    def c_fwd(r, side, zfirst, odd=0):
        if zfirst:
            rows = pl.ds(48 * side, 48 - 16 * side)
        else:
            rows = pl.ds(0, HALF) if side != odd else pl.ds(HALF, SET - HALF)
        return rdma(
            fwd_out.at[r, rows], fwd.at[r, rows], send_sem.at[4 + zfirst], fwd_sem.at[r], up if side == 0 else down
        )

    def c_rcv(r, side, zfirst):
        rows = pl.ds(0, HALF if zfirst else SET)
        return rdma(
            rcv_out.at[r, side, rows], rcv.at[r, side, rows],
            send_sem.at[6 + zfirst], rcv_sem.at[r], up if side == 0 else down,
        )

    def arrived(ref, sem):
        rdma(ref, ref, send_sem.at[4], sem, twin).wait_recv()

    def c_zr(r):
        return rdma(zr_out.at[r], zr.at[r], send_sem.at[8], zr_sem.at[r], far)

    def c_zf(q, r):
        return rdma(zf_out.at[q], zf.at[q], send_sem.at[9], zr_sem.at[r], far)

    def c_xr(r, d):
        return rdma(xr_out.at[r, d - 1], xr.at[r, d - 1], send_sem.at[10], xr_sem.at[r], at_col((col + d) % NB))

    def zfirst_of(r):
        return (r > RN) & (r < RN + 2 * ZROUNDS) & (r % 2 == 1)

    def both(stage, zstage):
        def run(r):
            pl.when(jnp.logical_not(zfirst_of(r)))(lambda: stage(r))
            pl.when(zfirst_of(r))(lambda: zstage(r, (r - RN) // 2))

        return run

    def mine(at):
        return pl.ds(pl.multiple_of(64 * zh + at, 16), 16)

    def others(at):
        return pl.ds(pl.multiple_of(64 * (1 - zh) + at, 16), 16)

    def make_block(c, d):
        b = (c + d) % NB
        direct = s_buf[c, :, b]
        if d == 0:
            return direct
        other = s_buf[b, :, c]
        mirrored = jnp.stack(
            [
                jnp.concatenate([other[0, :4], other[1, :4]], axis=0),
                jnp.concatenate([other[0, 4:], other[1, 4:]], axis=0),
            ]
        )
        return direct + mirrored

    def stage1(r, pairs):
        n = r % RN
        columns = pl.ds(pl.multiple_of(n * QN, QN), QN)
        for m in range(4):
            total = None
            for slot, e in pairs:
                lhs = g[slot, 2 * m : 2 * m + 2].reshape(256, 2048)
                part = jnp.dot(lhs, wt[e, :, columns], preferred_element_type=jnp.float32)
                total = part if total is None else total + part
            s_buf[2 * m : 2 * m + 2] = total.reshape(2, 2, 8, 8, QN)
        def form(store):
            for rel, yy in enumerate((yo, yp, ym, y)):
                at = 0
                for zz in range(2):
                    for d in range(5 - zz):
                        store(rel, pl.ds(at, 16), make_block(zz * 4 + yy, d).reshape(16, QN))
                        at += 16

        def form_y(r):
            def store(rel, rows, value):
                if rel == 0:
                    encode(fwd_out.at[r, rows], value)
                else:
                    t[r, rel - 1, rows] = value

            form(store)
            for odd in range(2):
                @pl.when(r % 2 == odd)
                def _(odd=odd):
                    c_fwd(r, 0, 0, odd).start()
                    c_fwd(r, 1, 0, odd).start()

        def form_z(r, q):
            def store(rel, rows, value):
                if rel == 0:
                    t_far[q, rows] = value
                else:
                    t[r, rel - 1, rows] = value

            form(store)
            for at in range(0, HALF, 16):
                encode(zf_out.at[q, 0, pl.ds(at, 16)], t_far[q, others(at)])
                for rel in range(3):
                    encode(zf_out.at[q, 1 + rel, pl.ds(at, 16)], t[r, rel, others(at)])
            c_zf(q, r).start()

        if len(pairs) == 1:
            form_y(r)
        else:
            both(form_y, form_z)(r)

    def stage2_y(r):
        arrived(fwd.at[r], fwd_sem.at[r])

        def pass_on(odd):
            for side in range(2):
                for at in range(0, SET, 16):
                    rows = pl.ds(at, 16)
                    value = t[r, side, rows]
                    if (at < HALF) == (side != odd):
                        value = value + decode(fwd.at[r, rows])
                    encode(rcv_out.at[r, side, rows], value)
                c_rcv(r, side, 0).start()

        for odd in range(2):
            pl.when(r % 2 == odd)(lambda odd=odd: pass_on(odd))

    def stage2_z(r, q):
        arrived(zf.at[q], zr_sem.at[r])
        for at in range(0, HALF, 16):
            rows = pl.ds(at, 16)
            encode(fwd_out.at[r, rows], t_far[q, mine(at)] + decode(zf.at[q, 0, rows]))
        c_fwd(r, 0, 1).start()
        c_fwd(r, 1, 1).start()
        for rel in range(3):
            for at in range(0, HALF, 16):
                t[r, rel, mine(at)] = t[r, rel, mine(at)] + decode(zf.at[q, 1 + rel, pl.ds(at, 16)])

    def stage3_y(r):
        arrived(rcv.at[r], rcv_sem.at[r])
        for at in range(0, SET, 16):
            rows = pl.ds(at, 16)
            t[r, 2, rows] = t[r, 2, rows] + decode(rcv.at[r, 0, rows]) + decode(rcv.at[r, 1, rows])
        for at in range(0, HALF, 16):
            encode(zr_out.at[r, pl.ds(at, 16)], t[r, 2, others(at)])
        c_zr(r).start()

    def stage3_z(r, q):
        arrived(fwd.at[r, pl.ds(0, HALF)], fwd_sem.at[r])
        for side in range(2):
            for at in range(0, HALF, 16):
                rows = pl.ds(at, 16)
                value = t[r, side, mine(at)]
                if (at >= 48) == (side == 1):
                    value = value + decode(fwd.at[r, rows])
                encode(rcv_out.at[r, side, rows], value)
            c_rcv(r, side, 1).start()

    def exchange(r):
        for d in range(1, 5):
            encode(xr_out.at[r, d - 1], f[r, d])
            if d < 4:
                c_xr(r, d).start()

        @pl.when(zh == 0)
        def _():
            c_xr(r, 4).start()

    def stage4_y(r):
        arrived(zr.at[r], zr_sem.at[r])
        own_rows = pl.ds(pl.multiple_of(HALF * zh, 16), 64)
        theirs = pl.ds(pl.multiple_of(16 * zh, 16), 64)
        f[r, 0:4] = (t[r, 2, own_rows] + decode(zr.at[r, theirs])).reshape(4, 16, QN)
        f[r, 4] = t[r, 2, pl.ds(64, 16)] + decode(zr.at[r, pl.ds(64, 16)])
        exchange(r)

    def stage4_z(r, q):
        arrived(rcv.at[r, :, pl.ds(0, HALF)], rcv_sem.at[r])
        for at in range(0, HALF, 16):
            rows = pl.ds(at, 16)
            t[r, 2, rows] = t[r, 2, mine(at)] + decode(rcv.at[r, 0, rows]) + decode(rcv.at[r, 1, rows])
        f[r, 0:4] = t[r, 2, pl.ds(pl.multiple_of(16 * zh, 16), 64)].reshape(4, 16, QN)
        f[r, 4] = t[r, 2, pl.ds(64, 16)]
        exchange(r)

    def stage5(r):
        @pl.when(zh == 0)
        def _():
            arrived(xr.at[r, 0:3], xr_sem.at[r])

        @pl.when(zh == 1)
        def _():
            arrived(xr.at[r], xr_sem.at[r])

        s, n = r // RN, r % RN
        columns = pl.ds(pl.multiple_of(n * QN, QN), QN)

        def place(block, b, swap):
            for i in range(4):
                for j in range(4):
                    p, q = (j, i) if swap else (i, j)
                    at = (p // 2) * 8 + (q // 2) * 4 + (p % 2) * 2 + q % 2
                    lad_ref[s, pl.ds(i * 32 + b * 4 + j, 1), columns] = block(at)

        def from_f(d):
            return lambda at: f[r, d, pl.ds(at, 1)]

        def from_xr(d):
            value = decode(xr.at[r, d - 1])
            return lambda at: value[at : at + 1]

        def at_of(p, q):
            return (p // 2) * 8 + (q // 2) * 4 + (p % 2) * 2 + q % 2

        for i in range(4):
            for j in range(4):
                lad_ref[s, pl.ds(i * 32 + col * 4 + j, 1), columns] = (
                    f[r, 0, pl.ds(at_of(i, j), 1)] + f[r, 0, pl.ds(at_of(j, i), 1)]
                )
        for d in range(1, 4):
            place(from_f(d), (col + d) % NB, False)
            place(from_xr(d), (col + NB - d) % NB, True)

        @pl.when(zh == 0)
        def _():
            place(from_f(4), (col + 4) % NB, False)

        @pl.when(zh == 1)
        def _():
            place(from_xr(4), (col + 4) % NB, True)

        @pl.when(n == RN - 1)
        def _():
            write(s).start()

    def write(s):
        return pltpu.make_async_copy(lad_ref.at[s], out_hbm.at[s], own_sem.at[s])

    stages = ((stage2_y, stage2_z), (stage3_y, stage3_z), (stage4_y, stage4_z), (stage5, None))

    send_own_z(0)
    send_own_x(0)
    pass_z(0)
    cz(2, own).start()
    send_own_z(1)
    pass_x(0, 0)
    straight(2)
    send_own_x(1)
    cx(0, lefts[1], 0, 1).wait_recv()
    ct(0, lefts[1]).start()
    cx(0, rights[1], 1, 1).wait_recv()
    ct(0, rights[1]).start()
    far_arrived(0, 0)
    cz(0, fars[0], 6).start()
    ct(0, fars[0]).start()
    straight_across(2, 0, own_z)
    straight_pass(2)
    pass_z(1)
    straight_across(0, 6, fars[1])
    load.wait()
    end_twin(0)

    def gather3():
        pass_x(1, 0)

    def gather4():
        straight_far(2)

    def gather6():
        straight_across(2, 1, lefts[1])
        pass_x(1, 1)
        straight_across(2, 2, rights[1])

    def gather8():
        pass_far(1)
        straight_across(2, 3, fars[1])
        end_twin(1)
        end_twin(2)

    def step(it, carry):
        for when, hook in ((1, gather3), (2, gather4), (4, gather6), (8, gather8)):
            pl.when(it == when)(hook)

        @pl.when(it < RN)
        def _():
            stage1(it, [(0, e_l)])

        @pl.when((it >= RN + GAP) & (it < ROUNDS + GAP))
        def _():
            one = it < 2 * RN + GAP
            stage1(it - GAP, [(1, jnp.where(one, e_ff, e_fs)), (2, jnp.where(one, e_sf, e_ss))])

        for n in range(4):
            stage, zstage = stages[n]
            lone_r, r, z_r = it - LONE_LAGS[n], it - GAP - LAGS[n], it - GAP - Z_LAGS[n]
            is_lone = (lone_r >= 0) & (lone_r < RN)
            is_pair = (r >= RN) & (r < ROUNDS)
            if zstage is None:
                pl.when(is_lone)(lambda: stage(lone_r))
                pl.when(is_pair)(lambda: stage(r))
            else:
                pl.when(is_lone)(lambda: stage(lone_r))
                pl.when(is_pair & jnp.logical_not(zfirst_of(r)))(lambda: stage(r))
                pl.when(zfirst_of(z_r))(lambda: zstage(z_r, (z_r - RN) // 2))

        return carry

    lax.fori_loop(0, ROUNDS + GAP + LAGS[-1], step, 0)

    end_sends()
    for slot in range(3):
        write(slot).wait()


def ladder_call(tile_pairs, amplitudes, integrals):
    dma = pltpu.SemaphoreType.DMA
    return pl.pallas_call(
        kernel,
        out_shape=jax.ShapeDtypeStruct((3, 128, 1024), jnp.float32),
        in_specs=[
            pl.BlockSpec(memory_space=pltpu.VMEM),
            pl.BlockSpec(memory_space=pl.ANY),
            pl.BlockSpec(memory_space=pl.ANY),
        ],
        out_specs=pl.BlockSpec(memory_space=pl.ANY),
        scratch_shapes=[
            pltpu.VMEM((3, NB, 2, 64, 2048), jnp.bfloat16),
            pltpu.VMEM((5, 2048, 1024), jnp.bfloat16),
            pltpu.VMEM((NB, 2, NB, 8, QN), jnp.float32),
            pltpu.VMEM((ROUNDS, 3, SET, QN), jnp.float32),
            pltpu.VMEM((ZROUNDS, SET, QN), jnp.float32),
            pltpu.VMEM((ROUNDS, SET, WIDE), jnp.bfloat16),
            pltpu.VMEM((ROUNDS, SET, WIDE), jnp.bfloat16),
            pltpu.VMEM((ROUNDS, 2, SET, WIDE), jnp.bfloat16),
            pltpu.VMEM((ROUNDS, 2, SET, WIDE), jnp.bfloat16),
            pltpu.VMEM((ZROUNDS, 4, HALF, WIDE), jnp.bfloat16),
            pltpu.VMEM((ZROUNDS, 4, HALF, WIDE), jnp.bfloat16),
            pltpu.VMEM((ROUNDS, HALF, WIDE), jnp.bfloat16),
            pltpu.VMEM((ROUNDS, HALF, WIDE), jnp.bfloat16),
            pltpu.VMEM((ROUNDS, 5, 16, QN), jnp.float32),
            pltpu.VMEM((ROUNDS, 4, 16, WIDE), jnp.bfloat16),
            pltpu.VMEM((ROUNDS, 4, 16, WIDE), jnp.bfloat16),
            pltpu.VMEM((3, 128, 1024), jnp.float32),
            pltpu.VMEM((3, 64, 2048), jnp.bfloat16),
            dma,
            dma((7,)),
            dma((3, 2, 2)),
            dma((3, 2)),
            dma((3,)),
            dma((ROUNDS,)),
            dma((ROUNDS,)),
            dma((ROUNDS,)),
            dma((ROUNDS,)),
            dma((11,)),
            dma((4,)),
        ],
        compiler_params=pltpu.CompilerParams(
            collective_id=0, has_side_effects=True, vmem_limit_bytes=60 << 20
        ),
        cost_estimate=pl.CostEstimate(flops=21_474_836_480, bytes_accessed=24 << 20, transcendentals=0),
    )(tile_pairs, amplitudes, integrals)


def finish(tp_ref, lad_hbm, drv_hbm, occ_ref, virt_ref, res_hbm, upd_hbm, lad_ref, drv_ref, res_ref, upd_ref, sem):
    row, col = lax.axis_index("row"), lax.axis_index("col")
    lone = read_pairs(tp_ref)[2]
    reads = []
    for tile in range(3):
        slot = jnp.where(lone == tile, 0, 1 + tile - jnp.where(lone < tile, 1, 0))
        reads.append(pltpu.make_async_copy(lad_hbm.at[slot], lad_ref.at[tile], sem.at[0, tile]))
        reads.append(pltpu.make_async_copy(drv_hbm.at[tile], drv_ref.at[tile], sem.at[1, tile]))
    for c in reads:
        c.start()
    lanes = occ_ref[...].reshape(1, 32)
    across = lax.broadcasted_iota(jnp.int32, (32, 32), 1)
    eye = lax.broadcasted_iota(jnp.int32, (32, 32), 0) == across
    second = jnp.sum(jnp.where(eye, jnp.broadcast_to(lanes, (32, 32)), 0.0), axis=1, keepdims=True)
    place = lax.broadcasted_iota(jnp.int32, (1, 128), 1)
    sums = []
    for i in range(4):
        here = jnp.sum(jnp.where(across[:1] == col * 4 + i, lanes, 0.0), axis=1, keepdims=True)
        sums.append(jnp.broadcast_to(here + second, (32, 128)))
    for tile in range(3):
        inner, outer = virt_ref[tile, 1:2, :], virt_ref[tile, 0:1, :]
        for c in range(8):
            lead = jnp.sum(jnp.where(place == row * 8 + c, outer, 0.0), axis=1, keepdims=True)
            virtual_pair = lead + inner
            for i in range(4):
                upd_ref[tile, pl.ds(i * 32, 32), pl.ds(c * 128, 128)] = 1.0 / (sums[i] - virtual_pair)
    writes = []
    for tile in range(3):
        reads[2 * tile].wait()
        reads[2 * tile + 1].wait()
        for i in range(4):
            rows = pl.ds(i * 32, 32)
            residual = drv_ref[tile, rows].astype(jnp.float32) + lad_ref[tile, rows]
            res_ref[tile, rows] = residual
            upd_ref[tile, rows] = residual * upd_ref[tile, rows]
        writes.append(pltpu.make_async_copy(res_ref.at[tile], res_hbm.at[tile], sem.at[2, tile]))
        writes.append(pltpu.make_async_copy(upd_ref.at[tile], upd_hbm.at[tile], sem.at[3, tile]))
        writes[-2].start()
        writes[-1].start()
    for c in writes:
        c.wait()


def body(amplitudes, integrals, tile_pairs, driving, occupied_energy, virtual_energy):
    pairs = tile_pairs.T
    ladder = ladder_call(pairs, amplitudes, integrals)
    vmem, anywhere = pl.BlockSpec(memory_space=pltpu.VMEM), pl.BlockSpec(memory_space=pl.ANY)
    out = jax.ShapeDtypeStruct(driving.shape, jnp.float32)
    held = pltpu.VMEM(driving.shape, jnp.float32)
    return pl.pallas_call(
        finish,
        out_shape=[out, out],
        in_specs=[vmem, anywhere, anywhere, vmem, vmem],
        out_specs=[anywhere, anywhere],
        scratch_shapes=[held, pltpu.VMEM(driving.shape, jnp.bfloat16), held, held, pltpu.SemaphoreType.DMA((4, 3))],
        compiler_params=pltpu.CompilerParams(vmem_limit_bytes=60 << 20),
    )(pairs, ladder, driving, occupied_energy, virtual_energy)


def solution(mesh):
    return jax.shard_map(
        body,
        mesh=mesh,
        in_specs=(
            P(None, "row", "col"),
            P(None, "col", "row"),
            P(),
            P(None, "col", "row"),
            P(),
            P(),
        ),
        out_specs=(P(None, "col", "row"), P(None, "col", "row")),
        check_vma=False,
    )
```

```python
import functools

import jax
import jax.numpy as jnp
from jax import lax
from jax.experimental import pallas as pl
from jax.experimental.pallas import tpu as pltpu
from jax.sharding import PartitionSpec as P

MESH = pl.DeviceIdType.MESH
NB = 8
QN = 256
RN = 4
ROUNDS = 12
SET = 144
HALF = 80
WIDE = QN + QN // 2
LEVELS = 10
LONE_LAGS, LAGS, Z_LAGS = (2, 7, 10, 14), (1, 3, 6, 9), (3, 4, 7, 9)
ZROUNDS = 1
GAP = 4


def encode(ref, value):
    lead = value.astype(jnp.bfloat16)
    wide = lead.astype(jnp.float32)
    safe = jnp.where(jnp.abs(wide) < 1e-36, 1.0, wide)
    steps = jnp.round((value - wide) * pl.reciprocal(safe, approx=True) * (256.0 * LEVELS))
    steps = jnp.clip(steps, -LEVELS, LEVELS)
    half = QN // 2
    ref[:, :QN] = lead
    ref[:, QN:] = (steps[:, :half] * (2 * LEVELS + 1) + steps[:, half:]).astype(jnp.bfloat16)


def decode(ref):
    wide = ref[:, :QN].astype(jnp.float32)
    code = ref[:, QN:].astype(jnp.float32)
    first = jnp.round(code * (1.0 / (2 * LEVELS + 1)))
    second = code - first * (2 * LEVELS + 1)
    return wide + wide * (jnp.concatenate([first, second], axis=1) * (1.0 / (256.0 * LEVELS)))


def read_pairs(tp_ref):
    pairs = tp_ref[...]
    src = [pairs[0, e] for e in range(5)]
    dst = [pairs[1, e] for e in range(5)]
    counts = [sum((src[e] == v).astype(jnp.int32) for e in range(5)) for v in range(3)]
    return src, dst, jnp.where(counts[0] == 1, 0, jnp.where(counts[1] == 1, 1, 2))


def kernel(
    tp_ref, amp_hbm, int_hbm, out_hbm,
    g, wt, s_buf, t, t_far, fwd_out, fwd, rcv_out, rcv, zf_out, zf, zr_out, zr, f, xr_out, xr, lad_ref, amp_ref,
    int_sem, z_sem, x_sem, f_sem, t_sem, fwd_sem, rcv_sem, zr_sem, xr_sem, send_sem, own_sem,
):
    row, col = lax.axis_index("row"), lax.axis_index("col")
    x, zl, k = row // 4, (row // 2) % 2, row % 2
    zh, y = col // 4, col % 4

    def at_row(xx, zz, kk):
        return (xx * 4 + zz * 2 + kk, col)

    def at_col(cc):
        return (row, cc)

    xp, xm, xo = (x + 1) % 4, (x + 3) % 4, (x + 2) % 4
    yp, ym, yo = (y + 1) % 4, (y + 3) % 4, (y + 2) % 4
    right, left = at_row(xp, zl, k), at_row(xm, zl, k)
    zpart, twin = at_row(x, 1 - zl, k), at_row(x, zl, 1 - k)
    up, down = at_col(zh * 4 + yp), at_col(zh * 4 + ym)
    far = at_col((1 - zh) * 4 + y)

    load_own = pltpu.make_async_copy(amp_hbm, amp_ref, own_sem.at[3])
    load_own.start()

    barrier = pltpu.get_barrier_semaphore()
    partners = [right, left, zpart, twin] + [at_col((col + d) % NB) for d in range(1, NB)]
    for p in partners:
        pl.semaphore_signal(barrier, inc=1, device_id=p, device_id_type=MESH)
    load = pltpu.make_async_copy(int_hbm, wt, int_sem)
    load.start()

    src, dst, lone = read_pairs(tp_ref)
    first = jnp.where(lone == 0, 1, 0)
    second = jnp.where(lone == 2, 1, 2)

    def entry(a, b):
        found = jnp.int32(0)
        for e in range(1, 5):
            found = jnp.where((src[e] == a) & (dst[e] == b), e, found)
        return found

    e_l = entry(lone, lone)
    e_ff, e_sf = entry(first, first), entry(second, first)
    e_fs, e_ss = entry(first, second), entry(second, second)

    own = x * 2 + zl
    to = lax.broadcasted_iota(jnp.int32, (64, 64), 0)
    frm = lax.broadcasted_iota(jnp.int32, (64, 64), 1)
    block, mid, low = to // 8, (to // 2) % 2, to % 2
    distance = (block + NB - own) % NB
    direct = (distance < 4) | ((distance == 4) & (block >= 4))
    ilo, jlo = jnp.where(direct, mid, low), jnp.where(direct, low, mid)
    order64 = (frm == ilo * 32 + block * 4 + ((to // 4) % 2) * 2 + jlo).astype(jnp.bfloat16)
    load_own.wait()
    for s, tile in ((0, lone), (2, second), (1, first)):
        g[s, own, k] = jnp.dot(order64, amp_ref[tile], preferred_element_type=jnp.float32).astype(jnp.bfloat16)
    pl.semaphore_wait(barrier, len(partners))

    def rdma(ref_src, ref_dst, ss, rs, dev):
        return pltpu.make_async_remote_copy(
            src_ref=ref_src, dst_ref=ref_dst, send_sem=ss, recv_sem=rs, device_id=dev, device_id_type=MESH
        )

    def chip(xx, zz):
        return xx * 2 + zz

    def cz(s, a, i=0):
        return rdma(g.at[s, a, k], g.at[s, a, k], send_sem.at[0], z_sem.at[s + i], zpart)

    def cx(s, a, side, which):
        return rdma(g.at[s, a, k], g.at[s, a, k], send_sem.at[1], x_sem.at[s, side, which], right if side == 0 else left)

    def cf(s, a, side, which):
        part = g.at[s, a, k, pl.ds(32 * side, 32)]
        return rdma(part, part, send_sem.at[2], f_sem.at[s, which], right if side == 0 else left)

    def far_arrived(s, which):
        whole = g.at[s, fars[which], k]
        rdma(whole, whole, send_sem.at[2], f_sem.at[s, which], right).wait_recv()

    def ct(s, a):
        return rdma(g.at[s, a, k], g.at[s, a, k], send_sem.at[3], t_sem.at[s], twin)

    own_z = chip(x, 1 - zl)
    lefts, rights = (chip(xm, zl), chip(xm, 1 - zl)), (chip(xp, zl), chip(xp, 1 - zl))
    fars = (chip(xo, zl), chip(xo, 1 - zl))

    def send_own_z(s):
        cz(s, own).start()

    def send_own_x(s):
        cx(s, own, 0, 0).start()
        cx(s, own, 1, 0).start()
        ct(s, own).start()

    def pass_z(s):
        cz(s, own_z).wait_recv()
        cx(s, own_z, 0, 1).start()
        cx(s, own_z, 1, 1).start()
        ct(s, own_z).start()

    def pass_x(s, which):
        cx(s, lefts[which], 0, which).wait_recv()
        cf(s, lefts[which], 0, which).start()
        ct(s, lefts[which]).start()
        cx(s, rights[which], 1, which).wait_recv()
        cf(s, rights[which], 1, which).start()
        ct(s, rights[which]).start()

    def pass_far(s):
        for which in range(2):
            far_arrived(s, which)
            ct(s, fars[which]).start()

    def end_twin(s):
        half = g.at[s, :, 1 - k]
        rdma(half, half, send_sem.at[3], t_sem.at[s], twin).wait_recv()

    def straight(s):
        cx(s, own, 0, 0).start()
        cx(s, own, 1, 0).start()
        ct(s, own).start()

    def straight_pass(s):
        cx(s, lefts[0], 0, 0).wait_recv()
        cf(s, lefts[0], 0, 0).start()
        cx(s, rights[0], 1, 0).wait_recv()
        cf(s, rights[0], 1, 0).start()
        cz(s, lefts[0], 1).start()
        cz(s, rights[0], 2).start()
        ct(s, lefts[0]).start()
        ct(s, rights[0]).start()

    def straight_far(s):
        far_arrived(s, 0)
        cz(s, fars[0], 3).start()
        ct(s, fars[0]).start()

    def straight_across(s, i, a):
        cz(s, a, i).wait_recv()
        ct(s, a).start()

    def sent(ref, i):
        rdma(ref, ref, send_sem.at[i], z_sem.at[0], twin).wait_send()

    def end_sends():
        sent(g.at[0, 0:7, 0], 0)
        sent(g.at[0, 0:5], 1)
        sent(g.at[0, 0:2], 2)
        sent(g.at[:, :, 0], 3)
        sent(fwd_out.at[0 : ROUNDS - ZROUNDS], 4)
        sent(fwd_out.at[0:ZROUNDS, pl.ds(0, HALF)], 5)
        sent(rcv_out.at[0 : ROUNDS - ZROUNDS], 6)
        sent(rcv_out.at[0:ZROUNDS, :, pl.ds(0, HALF)], 7)
        sent(zr.at[0 : ROUNDS - ZROUNDS], 8)
        sent(zf_out, 9)

        @pl.when(zh == 0)
        def _():
            sent(xr_out, 10)

        @pl.when(zh == 1)
        def _():
            sent(xr_out.at[:, 0:3], 10)

    def c_fwd(r, side, zfirst, odd=0):
        if zfirst:
            rows = pl.ds(48 * side, 48 - 16 * side)
        else:
            rows = pl.ds(0, HALF) if side != odd else pl.ds(HALF, SET - HALF)
        return rdma(
            fwd_out.at[r, rows], fwd.at[r, rows], send_sem.at[4 + zfirst], fwd_sem.at[r], up if side == 0 else down
        )

    def c_rcv(r, side, zfirst):
        rows = pl.ds(0, HALF if zfirst else SET)
        return rdma(
            rcv_out.at[r, side, rows], rcv.at[r, side, rows],
            send_sem.at[6 + zfirst], rcv_sem.at[r], up if side == 0 else down,
        )

    def arrived(ref, sem):
        rdma(ref, ref, send_sem.at[4], sem, twin).wait_recv()

    def c_zr(r):
        return rdma(zr_out.at[r], zr.at[r], send_sem.at[8], zr_sem.at[r], far)

    def c_zf(q, r):
        return rdma(zf_out.at[q], zf.at[q], send_sem.at[9], zr_sem.at[r], far)

    def c_xr(r, d):
        return rdma(xr_out.at[r, d - 1], xr.at[r, d - 1], send_sem.at[10], xr_sem.at[r], at_col((col + d) % NB))

    def zfirst_of(r):
        return (r > RN) & (r < RN + 2 * ZROUNDS) & (r % 2 == 1)

    def both(stage, zstage):
        def run(r):
            pl.when(jnp.logical_not(zfirst_of(r)))(lambda: stage(r))
            pl.when(zfirst_of(r))(lambda: zstage(r, (r - RN) // 2))

        return run

    def mine(at):
        return pl.ds(pl.multiple_of(64 * zh + at, 16), 16)

    def others(at):
        return pl.ds(pl.multiple_of(64 * (1 - zh) + at, 16), 16)

    def make_block(c, d):
        b = (c + d) % NB
        direct = s_buf[c, :, b]
        if d == 0:
            return direct
        other = s_buf[b, :, c]
        mirrored = jnp.stack(
            [
                jnp.concatenate([other[0, :4], other[1, :4]], axis=0),
                jnp.concatenate([other[0, 4:], other[1, 4:]], axis=0),
            ]
        )
        return direct + mirrored

    def stage1(r, pairs):
        n = r % RN
        columns = pl.ds(pl.multiple_of(n * QN, QN), QN)
        for m in range(4):
            total = None
            for slot, e in pairs:
                lhs = g[slot, 2 * m : 2 * m + 2].reshape(256, 2048)
                part = jnp.dot(lhs, wt[e, :, columns], preferred_element_type=jnp.float32)
                total = part if total is None else total + part
            s_buf[2 * m : 2 * m + 2] = total.reshape(2, 2, 8, 8, QN)
        def form(store):
            for rel, yy in enumerate((yo, yp, ym, y)):
                at = 0
                for zz in range(2):
                    for d in range(5 - zz):
                        store(rel, pl.ds(at, 16), make_block(zz * 4 + yy, d).reshape(16, QN))
                        at += 16

        def form_y(r):
            def store(rel, rows, value):
                if rel == 0:
                    encode(fwd_out.at[r, rows], value)
                else:
                    t[r, rel - 1, rows] = value

            form(store)
            for odd in range(2):
                @pl.when(r % 2 == odd)
                def _(odd=odd):
                    c_fwd(r, 0, 0, odd).start()
                    c_fwd(r, 1, 0, odd).start()

        def form_z(r, q):
            def store(rel, rows, value):
                if rel == 0:
                    t_far[q, rows] = value
                else:
                    t[r, rel - 1, rows] = value

            form(store)
            for at in range(0, HALF, 16):
                encode(zf_out.at[q, 0, pl.ds(at, 16)], t_far[q, others(at)])
                for rel in range(3):
                    encode(zf_out.at[q, 1 + rel, pl.ds(at, 16)], t[r, rel, others(at)])
            c_zf(q, r).start()

        if len(pairs) == 1:
            form_y(r)
        else:
            both(form_y, form_z)(r)

    def stage2_y(r):
        arrived(fwd.at[r], fwd_sem.at[r])

        def pass_on(odd):
            for side in range(2):
                for at in range(0, SET, 16):
                    rows = pl.ds(at, 16)
                    value = t[r, side, rows]
                    if (at < HALF) == (side != odd):
                        value = value + decode(fwd.at[r, rows])
                    encode(rcv_out.at[r, side, rows], value)
                c_rcv(r, side, 0).start()

        for odd in range(2):
            pl.when(r % 2 == odd)(lambda odd=odd: pass_on(odd))

    def stage2_z(r, q):
        arrived(zf.at[q], zr_sem.at[r])
        for at in range(0, HALF, 16):
            rows = pl.ds(at, 16)
            encode(fwd_out.at[r, rows], t_far[q, mine(at)] + decode(zf.at[q, 0, rows]))
        c_fwd(r, 0, 1).start()
        c_fwd(r, 1, 1).start()
        for rel in range(3):
            for at in range(0, HALF, 16):
                t[r, rel, mine(at)] = t[r, rel, mine(at)] + decode(zf.at[q, 1 + rel, pl.ds(at, 16)])

    def stage3_y(r):
        arrived(rcv.at[r], rcv_sem.at[r])
        for at in range(0, SET, 16):
            rows = pl.ds(at, 16)
            t[r, 2, rows] = t[r, 2, rows] + decode(rcv.at[r, 0, rows]) + decode(rcv.at[r, 1, rows])
        for at in range(0, HALF, 16):
            encode(zr_out.at[r, pl.ds(at, 16)], t[r, 2, others(at)])
        c_zr(r).start()

    def stage3_z(r, q):
        arrived(fwd.at[r, pl.ds(0, HALF)], fwd_sem.at[r])
        for side in range(2):
            for at in range(0, HALF, 16):
                rows = pl.ds(at, 16)
                value = t[r, side, mine(at)]
                if (at >= 48) == (side == 1):
                    value = value + decode(fwd.at[r, rows])
                encode(rcv_out.at[r, side, rows], value)
            c_rcv(r, side, 1).start()

    def exchange(r):
        for d in range(1, 5):
            encode(xr_out.at[r, d - 1], f[r, d])
            if d < 4:
                c_xr(r, d).start()

        @pl.when(zh == 0)
        def _():
            c_xr(r, 4).start()

    def stage4_y(r):
        arrived(zr.at[r], zr_sem.at[r])
        own_rows = pl.ds(pl.multiple_of(HALF * zh, 16), 64)
        theirs = pl.ds(pl.multiple_of(16 * zh, 16), 64)
        f[r, 0:4] = (t[r, 2, own_rows] + decode(zr.at[r, theirs])).reshape(4, 16, QN)
        f[r, 4] = t[r, 2, pl.ds(64, 16)] + decode(zr.at[r, pl.ds(64, 16)])
        exchange(r)

    def stage4_z(r, q):
        arrived(rcv.at[r, :, pl.ds(0, HALF)], rcv_sem.at[r])
        for at in range(0, HALF, 16):
            rows = pl.ds(at, 16)
            t[r, 2, rows] = t[r, 2, mine(at)] + decode(rcv.at[r, 0, rows]) + decode(rcv.at[r, 1, rows])
        f[r, 0:4] = t[r, 2, pl.ds(pl.multiple_of(16 * zh, 16), 64)].reshape(4, 16, QN)
        f[r, 4] = t[r, 2, pl.ds(64, 16)]
        exchange(r)

    def stage5(r):
        @pl.when(zh == 0)
        def _():
            arrived(xr.at[r, 0:3], xr_sem.at[r])

        @pl.when(zh == 1)
        def _():
            arrived(xr.at[r], xr_sem.at[r])

        s, n = r // RN, r % RN
        columns = pl.ds(pl.multiple_of(n * QN, QN), QN)

        def place(block, b, swap):
            for i in range(4):
                for j in range(4):
                    p, q = (j, i) if swap else (i, j)
                    at = (p // 2) * 8 + (q // 2) * 4 + (p % 2) * 2 + q % 2
                    lad_ref[s, pl.ds(i * 32 + b * 4 + j, 1), columns] = block(at)

        def from_f(d):
            return lambda at: f[r, d, pl.ds(at, 1)]

        def from_xr(d):
            value = decode(xr.at[r, d - 1])
            return lambda at: value[at : at + 1]

        def at_of(p, q):
            return (p // 2) * 8 + (q // 2) * 4 + (p % 2) * 2 + q % 2

        for i in range(4):
            for j in range(4):
                lad_ref[s, pl.ds(i * 32 + col * 4 + j, 1), columns] = (
                    f[r, 0, pl.ds(at_of(i, j), 1)] + f[r, 0, pl.ds(at_of(j, i), 1)]
                )
        for d in range(1, 4):
            place(from_f(d), (col + d) % NB, False)
            place(from_xr(d), (col + NB - d) % NB, True)

        @pl.when(zh == 0)
        def _():
            place(from_f(4), (col + 4) % NB, False)

        @pl.when(zh == 1)
        def _():
            place(from_xr(4), (col + 4) % NB, True)

        @pl.when(n == RN - 1)
        def _():
            write(s).start()

    def write(s):
        return pltpu.make_async_copy(lad_ref.at[s], out_hbm.at[s], own_sem.at[s])

    stages = ((stage2_y, stage2_z), (stage3_y, stage3_z), (stage4_y, stage4_z), (stage5, None))

    send_own_z(0)
    send_own_x(0)
    pass_z(0)
    cz(2, own).start()
    send_own_z(1)
    pass_x(0, 0)
    straight(2)
    send_own_x(1)
    cx(0, lefts[1], 0, 1).wait_recv()
    ct(0, lefts[1]).start()
    cx(0, rights[1], 1, 1).wait_recv()
    ct(0, rights[1]).start()
    far_arrived(0, 0)
    cz(0, fars[0], 6).start()
    ct(0, fars[0]).start()
    straight_across(2, 0, own_z)
    straight_pass(2)
    pass_z(1)
    straight_across(0, 6, fars[1])
    load.wait()
    end_twin(0)

    def gather3():
        pass_x(1, 0)

    def gather4():
        straight_far(2)

    def gather6():
        straight_across(2, 1, lefts[1])
        pass_x(1, 1)
        straight_across(2, 2, rights[1])

    def gather8():
        pass_far(1)
        straight_across(2, 3, fars[1])
        end_twin(1)
        end_twin(2)

    def step(it, carry):
        for when, hook in ((1, gather3), (2, gather4), (4, gather6), (8, gather8)):
            pl.when(it == when)(hook)

        @pl.when(it < RN)
        def _():
            stage1(it, [(0, e_l)])

        @pl.when((it >= RN + GAP) & (it < ROUNDS + GAP))
        def _():
            one = it < 2 * RN + GAP
            stage1(it - GAP, [(1, jnp.where(one, e_ff, e_fs)), (2, jnp.where(one, e_sf, e_ss))])

        for n in range(4):
            stage, zstage = stages[n]
            lone_r, r, z_r = it - LONE_LAGS[n], it - GAP - LAGS[n], it - GAP - Z_LAGS[n]
            is_lone = (lone_r >= 0) & (lone_r < RN)
            is_pair = (r >= RN) & (r < ROUNDS)
            if zstage is None:
                pl.when(is_lone)(lambda: stage(lone_r))
                pl.when(is_pair)(lambda: stage(r))
            else:
                pl.when(is_lone)(lambda: stage(lone_r))
                pl.when(is_pair & jnp.logical_not(zfirst_of(r)))(lambda: stage(r))
                pl.when(zfirst_of(z_r))(lambda: zstage(z_r, (z_r - RN) // 2))

        return carry

    lax.fori_loop(0, ROUNDS + GAP + LAGS[-1], step, 0)

    end_sends()
    for slot in range(3):
        write(slot).wait()


def ladder_call(tile_pairs, amplitudes, integrals):
    dma = pltpu.SemaphoreType.DMA
    return pl.pallas_call(
        kernel,
        out_shape=jax.ShapeDtypeStruct((3, 128, 1024), jnp.float32),
        in_specs=[
            pl.BlockSpec(memory_space=pltpu.VMEM),
            pl.BlockSpec(memory_space=pl.ANY),
            pl.BlockSpec(memory_space=pl.ANY),
        ],
        out_specs=pl.BlockSpec(memory_space=pl.ANY),
        scratch_shapes=[
            pltpu.VMEM((3, NB, 2, 64, 2048), jnp.bfloat16),
            pltpu.VMEM((5, 2048, 1024), jnp.bfloat16),
            pltpu.VMEM((NB, 2, NB, 8, QN), jnp.float32),
            pltpu.VMEM((ROUNDS, 3, SET, QN), jnp.float32),
            pltpu.VMEM((ZROUNDS, SET, QN), jnp.float32),
            pltpu.VMEM((ROUNDS, SET, WIDE), jnp.bfloat16),
            pltpu.VMEM((ROUNDS, SET, WIDE), jnp.bfloat16),
            pltpu.VMEM((ROUNDS, 2, SET, WIDE), jnp.bfloat16),
            pltpu.VMEM((ROUNDS, 2, SET, WIDE), jnp.bfloat16),
            pltpu.VMEM((ZROUNDS, 4, HALF, WIDE), jnp.bfloat16),
            pltpu.VMEM((ZROUNDS, 4, HALF, WIDE), jnp.bfloat16),
            pltpu.VMEM((ROUNDS, HALF, WIDE), jnp.bfloat16),
            pltpu.VMEM((ROUNDS, HALF, WIDE), jnp.bfloat16),
            pltpu.VMEM((ROUNDS, 5, 16, QN), jnp.float32),
            pltpu.VMEM((ROUNDS, 4, 16, WIDE), jnp.bfloat16),
            pltpu.VMEM((ROUNDS, 4, 16, WIDE), jnp.bfloat16),
            pltpu.VMEM((3, 128, 1024), jnp.float32),
            pltpu.VMEM((3, 64, 2048), jnp.bfloat16),
            dma,
            dma((7,)),
            dma((3, 2, 2)),
            dma((3, 2)),
            dma((3,)),
            dma((ROUNDS,)),
            dma((ROUNDS,)),
            dma((ROUNDS,)),
            dma((ROUNDS,)),
            dma((11,)),
            dma((4,)),
        ],
        compiler_params=pltpu.CompilerParams(
            collective_id=0, has_side_effects=True, vmem_limit_bytes=60 << 20
        ),
        cost_estimate=pl.CostEstimate(flops=21_474_836_480, bytes_accessed=24 << 20, transcendentals=0),
    )(tile_pairs, amplitudes, integrals)


def finish(tp_ref, lad_hbm, drv_hbm, occ_ref, virt_ref, res_hbm, upd_hbm, lad_ref, drv_ref, res_ref, upd_ref, sem):
    row, col = lax.axis_index("row"), lax.axis_index("col")
    lone = read_pairs(tp_ref)[2]
    reads = []
    for tile in range(3):
        slot = jnp.where(lone == tile, 0, 1 + tile - jnp.where(lone < tile, 1, 0))
        reads.append(pltpu.make_async_copy(lad_hbm.at[slot], lad_ref.at[tile], sem.at[0, tile]))
        reads.append(pltpu.make_async_copy(drv_hbm.at[tile], drv_ref.at[tile], sem.at[1, tile]))
    for c in reads:
        c.start()
    lanes = occ_ref[...].reshape(1, 32)
    across = lax.broadcasted_iota(jnp.int32, (32, 32), 1)
    eye = lax.broadcasted_iota(jnp.int32, (32, 32), 0) == across
    second = jnp.sum(jnp.where(eye, jnp.broadcast_to(lanes, (32, 32)), 0.0), axis=1, keepdims=True)
    place = lax.broadcasted_iota(jnp.int32, (1, 128), 1)
    sums = []
    for i in range(4):
        here = jnp.sum(jnp.where(across[:1] == col * 4 + i, lanes, 0.0), axis=1, keepdims=True)
        sums.append(jnp.broadcast_to(here + second, (32, 128)))
    for tile in range(3):
        inner, outer = virt_ref[tile, 1:2, :], virt_ref[tile, 0:1, :]
        for c in range(8):
            lead = jnp.sum(jnp.where(place == row * 8 + c, outer, 0.0), axis=1, keepdims=True)
            virtual_pair = lead + inner
            for i in range(4):
                upd_ref[tile, pl.ds(i * 32, 32), pl.ds(c * 128, 128)] = 1.0 / (sums[i] - virtual_pair)
    writes = []
    for tile in range(3):
        reads[2 * tile].wait()
        reads[2 * tile + 1].wait()
        for i in range(4):
            rows = pl.ds(i * 32, 32)
            residual = drv_ref[tile, rows].astype(jnp.float32) + lad_ref[tile, rows]
            res_ref[tile, rows] = residual
            upd_ref[tile, rows] = residual * upd_ref[tile, rows]
        writes.append(pltpu.make_async_copy(res_ref.at[tile], res_hbm.at[tile], sem.at[2, tile]))
        writes.append(pltpu.make_async_copy(upd_ref.at[tile], upd_hbm.at[tile], sem.at[3, tile]))
        writes[-2].start()
        writes[-1].start()
    for c in writes:
        c.wait()


def body(amplitudes, integrals, tile_pairs, driving, occupied_energy, virtual_energy):
    pairs = tile_pairs.T
    ladder = ladder_call(pairs, amplitudes, integrals)
    vmem, anywhere = pl.BlockSpec(memory_space=pltpu.VMEM), pl.BlockSpec(memory_space=pl.ANY)
    out = jax.ShapeDtypeStruct(driving.shape, jnp.float32)
    held = pltpu.VMEM(driving.shape, jnp.float32)
    return pl.pallas_call(
        finish,
        out_shape=[out, out],
        in_specs=[vmem, anywhere, anywhere, vmem, vmem],
        out_specs=[anywhere, anywhere],
        scratch_shapes=[held, pltpu.VMEM(driving.shape, jnp.bfloat16), held, held, pltpu.SemaphoreType.DMA((4, 3))],
        compiler_params=pltpu.CompilerParams(vmem_limit_bytes=60 << 20),
    )(pairs, ladder, driving, occupied_energy, virtual_energy)


def solution(mesh):
    return jax.shard_map(
        body,
        mesh=mesh,
        in_specs=(
            P(None, "row", "col"),
            P(None, "col", "row"),
            P(),
            P(None, "col", "row"),
            P(),
            P(),
        ),
        out_specs=(P(None, "col", "row"), P(None, "col", "row")),
        check_vma=False,
    )
```

```python
import functools

import jax
import jax.numpy as jnp
from jax import lax
from jax.experimental import pallas as pl
from jax.experimental.pallas import tpu as pltpu
from jax.sharding import PartitionSpec as P

MESH = pl.DeviceIdType.MESH
NB = 8
QN = 256
RN = 4
ROUNDS = 12
SET = 144
HALF = 80
WIDE = QN + QN // 2
LEVELS = 10
LONE_LAGS, LAGS, Z_LAGS = (2, 7, 10, 14), (1, 3, 6, 9), (3, 4, 7, 9)
ZROUNDS = 1
GAP = 4


def encode(ref, value):
    lead = value.astype(jnp.bfloat16)
    wide = lead.astype(jnp.float32)
    safe = jnp.where(jnp.abs(wide) < 1e-36, 1.0, wide)
    steps = jnp.round((value - wide) * pl.reciprocal(safe, approx=True) * (256.0 * LEVELS))
    steps = jnp.clip(steps, -LEVELS, LEVELS)
    half = QN // 2
    ref[:, :QN] = lead
    ref[:, QN:] = (steps[:, :half] * (2 * LEVELS + 1) + steps[:, half:]).astype(jnp.bfloat16)


def decode(ref):
    wide = ref[:, :QN].astype(jnp.float32)
    code = ref[:, QN:].astype(jnp.float32)
    first = jnp.round(code * (1.0 / (2 * LEVELS + 1)))
    second = code - first * (2 * LEVELS + 1)
    return wide + wide * (jnp.concatenate([first, second], axis=1) * (1.0 / (256.0 * LEVELS)))


def read_pairs(tp_ref):
    pairs = tp_ref[...]
    src = [pairs[0, e] for e in range(5)]
    dst = [pairs[1, e] for e in range(5)]
    counts = [sum((src[e] == v).astype(jnp.int32) for e in range(5)) for v in range(3)]
    return src, dst, jnp.where(counts[0] == 1, 0, jnp.where(counts[1] == 1, 1, 2))


def kernel(
    tp_ref, amp_hbm, int_hbm, out_hbm,
    g, wt, s_buf, t, t_far, fwd_out, fwd, rcv_out, rcv, zf_out, zf, zr_out, zr, f, xr_out, xr, lad_ref, amp_ref,
    int_sem, z_sem, x_sem, f_sem, t_sem, fwd_sem, rcv_sem, zr_sem, xr_sem, send_sem, own_sem,
):
    row, col = lax.axis_index("row"), lax.axis_index("col")
    x, zl, k = row // 4, (row // 2) % 2, row % 2
    zh, y = col // 4, col % 4

    def at_row(xx, zz, kk):
        return (xx * 4 + zz * 2 + kk, col)

    def at_col(cc):
        return (row, cc)

    xp, xm, xo = (x + 1) % 4, (x + 3) % 4, (x + 2) % 4
    yp, ym, yo = (y + 1) % 4, (y + 3) % 4, (y + 2) % 4
    right, left = at_row(xp, zl, k), at_row(xm, zl, k)
    zpart, twin = at_row(x, 1 - zl, k), at_row(x, zl, 1 - k)
    up, down = at_col(zh * 4 + yp), at_col(zh * 4 + ym)
    far = at_col((1 - zh) * 4 + y)

    load_own = pltpu.make_async_copy(amp_hbm, amp_ref, own_sem.at[3])
    load_own.start()

    barrier = pltpu.get_barrier_semaphore()
    partners = [right, left, zpart, twin] + [at_col((col + d) % NB) for d in range(1, NB)]
    for p in partners:
        pl.semaphore_signal(barrier, inc=1, device_id=p, device_id_type=MESH)
    load = pltpu.make_async_copy(int_hbm, wt, int_sem)
    load.start()

    src, dst, lone = read_pairs(tp_ref)
    first = jnp.where(lone == 0, 1, 0)
    second = jnp.where(lone == 2, 1, 2)

    def entry(a, b):
        found = jnp.int32(0)
        for e in range(1, 5):
            found = jnp.where((src[e] == a) & (dst[e] == b), e, found)
        return found

    e_l = entry(lone, lone)
    e_ff, e_sf = entry(first, first), entry(second, first)
    e_fs, e_ss = entry(first, second), entry(second, second)

    own = x * 2 + zl
    to = lax.broadcasted_iota(jnp.int32, (64, 64), 0)
    frm = lax.broadcasted_iota(jnp.int32, (64, 64), 1)
    block, mid, low = to // 8, (to // 2) % 2, to % 2
    distance = (block + NB - own) % NB
    direct = (distance < 4) | ((distance == 4) & (block >= 4))
    ilo, jlo = jnp.where(direct, mid, low), jnp.where(direct, low, mid)
    order64 = (frm == ilo * 32 + block * 4 + ((to // 4) % 2) * 2 + jlo).astype(jnp.bfloat16)
    load_own.wait()
    for s, tile in ((0, lone), (2, second), (1, first)):
        g[s, own, k] = jnp.dot(order64, amp_ref[tile], preferred_element_type=jnp.float32).astype(jnp.bfloat16)
    pl.semaphore_wait(barrier, len(partners))

    def rdma(ref_src, ref_dst, ss, rs, dev):
        return pltpu.make_async_remote_copy(
            src_ref=ref_src, dst_ref=ref_dst, send_sem=ss, recv_sem=rs, device_id=dev, device_id_type=MESH
        )

    def chip(xx, zz):
        return xx * 2 + zz

    def cz(s, a, i=0):
        return rdma(g.at[s, a, k], g.at[s, a, k], send_sem.at[0], z_sem.at[s + i], zpart)

    def cx(s, a, side, which):
        return rdma(g.at[s, a, k], g.at[s, a, k], send_sem.at[1], x_sem.at[s, side, which], right if side == 0 else left)

    def cf(s, a, side, which):
        part = g.at[s, a, k, pl.ds(32 * side, 32)]
        return rdma(part, part, send_sem.at[2], f_sem.at[s, which], right if side == 0 else left)

    def far_arrived(s, which):
        whole = g.at[s, fars[which], k]
        rdma(whole, whole, send_sem.at[2], f_sem.at[s, which], right).wait_recv()

    def ct(s, a):
        return rdma(g.at[s, a, k], g.at[s, a, k], send_sem.at[3], t_sem.at[s], twin)

    own_z = chip(x, 1 - zl)
    lefts, rights = (chip(xm, zl), chip(xm, 1 - zl)), (chip(xp, zl), chip(xp, 1 - zl))
    fars = (chip(xo, zl), chip(xo, 1 - zl))

    def send_own_z(s):
        cz(s, own).start()

    def send_own_x(s):
        cx(s, own, 0, 0).start()
        cx(s, own, 1, 0).start()
        ct(s, own).start()

    def pass_z(s):
        cz(s, own_z).wait_recv()
        cx(s, own_z, 0, 1).start()
        cx(s, own_z, 1, 1).start()
        ct(s, own_z).start()

    def pass_x(s, which):
        cx(s, lefts[which], 0, which).wait_recv()
        cf(s, lefts[which], 0, which).start()
        ct(s, lefts[which]).start()
        cx(s, rights[which], 1, which).wait_recv()
        cf(s, rights[which], 1, which).start()
        ct(s, rights[which]).start()

    def pass_far(s):
        for which in range(2):
            far_arrived(s, which)
            ct(s, fars[which]).start()

    def end_twin(s):
        half = g.at[s, :, 1 - k]
        rdma(half, half, send_sem.at[3], t_sem.at[s], twin).wait_recv()

    def straight(s):
        cx(s, own, 0, 0).start()
        cx(s, own, 1, 0).start()
        ct(s, own).start()

    def straight_pass(s):
        cx(s, lefts[0], 0, 0).wait_recv()
        cf(s, lefts[0], 0, 0).start()
        cx(s, rights[0], 1, 0).wait_recv()
        cf(s, rights[0], 1, 0).start()
        cz(s, lefts[0], 1).start()
        cz(s, rights[0], 2).start()
        ct(s, lefts[0]).start()
        ct(s, rights[0]).start()

    def straight_far(s):
        far_arrived(s, 0)
        cz(s, fars[0], 3).start()
        ct(s, fars[0]).start()

    def straight_across(s, i, a):
        cz(s, a, i).wait_recv()
        ct(s, a).start()

    def sent(ref, i):
        rdma(ref, ref, send_sem.at[i], z_sem.at[0], twin).wait_send()

    def end_sends():
        sent(g.at[0, 0:7, 0], 0)
        sent(g.at[0, 0:5], 1)
        sent(g.at[0, 0:2], 2)
        sent(g.at[:, :, 0], 3)
        sent(fwd_out.at[0 : ROUNDS - ZROUNDS], 4)
        sent(fwd_out.at[0:ZROUNDS, pl.ds(0, HALF)], 5)
        sent(rcv_out.at[0 : ROUNDS - ZROUNDS], 6)
        sent(rcv_out.at[0:ZROUNDS, :, pl.ds(0, HALF)], 7)
        sent(zr.at[0 : ROUNDS - ZROUNDS], 8)
        sent(zf_out, 9)

        @pl.when(zh == 0)
        def _():
            sent(xr_out, 10)

        @pl.when(zh == 1)
        def _():
            sent(xr_out.at[:, 0:3], 10)

    def c_fwd(r, side, zfirst, odd=0):
        if zfirst:
            rows = pl.ds(48 * side, 48 - 16 * side)
        else:
            rows = pl.ds(0, HALF) if side != odd else pl.ds(HALF, SET - HALF)
        return rdma(
            fwd_out.at[r, rows], fwd.at[r, rows], send_sem.at[4 + zfirst], fwd_sem.at[r], up if side == 0 else down
        )

    def c_rcv(r, side, zfirst):
        rows = pl.ds(0, HALF if zfirst else SET)
        return rdma(
            rcv_out.at[r, side, rows], rcv.at[r, side, rows],
            send_sem.at[6 + zfirst], rcv_sem.at[r], up if side == 0 else down,
        )

    def arrived(ref, sem):
        rdma(ref, ref, send_sem.at[4], sem, twin).wait_recv()

    def c_zr(r):
        return rdma(zr_out.at[r], zr.at[r], send_sem.at[8], zr_sem.at[r], far)

    def c_zf(q, r):
        return rdma(zf_out.at[q], zf.at[q], send_sem.at[9], zr_sem.at[r], far)

    def c_xr(r, d):
        return rdma(xr_out.at[r, d - 1], xr.at[r, d - 1], send_sem.at[10], xr_sem.at[r], at_col((col + d) % NB))

    def zfirst_of(r):
        return (r > RN) & (r < RN + 2 * ZROUNDS) & (r % 2 == 1)

    def both(stage, zstage):
        def run(r):
            pl.when(jnp.logical_not(zfirst_of(r)))(lambda: stage(r))
            pl.when(zfirst_of(r))(lambda: zstage(r, (r - RN) // 2))

        return run

    def mine(at):
        return pl.ds(pl.multiple_of(64 * zh + at, 16), 16)

    def others(at):
        return pl.ds(pl.multiple_of(64 * (1 - zh) + at, 16), 16)

    def make_block(c, d):
        b = (c + d) % NB
        direct = s_buf[c, :, b]
        if d == 0:
            return direct
        other = s_buf[b, :, c]
        mirrored = jnp.stack(
            [
                jnp.concatenate([other[0, :4], other[1, :4]], axis=0),
                jnp.concatenate([other[0, 4:], other[1, 4:]], axis=0),
            ]
        )
        return direct + mirrored

    def stage1(r, pairs):
        n = r % RN
        columns = pl.ds(pl.multiple_of(n * QN, QN), QN)
        for m in range(4):
            total = None
            for slot, e in pairs:
                lhs = g[slot, 2 * m : 2 * m + 2].reshape(256, 2048)
                part = jnp.dot(lhs, wt[e, :, columns], preferred_element_type=jnp.float32)
                total = part if total is None else total + part
            s_buf[2 * m : 2 * m + 2] = total.reshape(2, 2, 8, 8, QN)
        def form(store, after_far=lambda: None):
            for rel, yy in enumerate((yo, yp, ym, y)):
                at = 0
                for zz in range(2):
                    for d in range(5 - zz):
                        store(rel, pl.ds(at, 16), make_block(zz * 4 + yy, d).reshape(16, QN))
                        at += 16
                if rel == 0:
                    after_far()

        def form_y(r):
            def store(rel, rows, value):
                if rel == 0:
                    encode(fwd_out.at[r, rows], value)
                else:
                    t[r, rel - 1, rows] = value

            def send():
                for odd in range(2):
                    @pl.when(r % 2 == odd)
                    def _(odd=odd):
                        c_fwd(r, 0, 0, odd).start()
                        c_fwd(r, 1, 0, odd).start()

            form(store, send)

        def form_z(r, q):
            def store(rel, rows, value):
                if rel == 0:
                    t_far[q, rows] = value
                else:
                    t[r, rel - 1, rows] = value

            form(store)
            for at in range(0, HALF, 16):
                encode(zf_out.at[q, 0, pl.ds(at, 16)], t_far[q, others(at)])
                for rel in range(3):
                    encode(zf_out.at[q, 1 + rel, pl.ds(at, 16)], t[r, rel, others(at)])
            c_zf(q, r).start()

        if len(pairs) == 1:
            form_y(r)
        else:
            both(form_y, form_z)(r)

    def stage2_y(r):
        arrived(fwd.at[r], fwd_sem.at[r])

        def pass_on(odd):
            for side in range(2):
                for at in range(0, SET, 16):
                    rows = pl.ds(at, 16)
                    value = t[r, side, rows]
                    if (at < HALF) == (side != odd):
                        value = value + decode(fwd.at[r, rows])
                    encode(rcv_out.at[r, side, rows], value)
                c_rcv(r, side, 0).start()

        for odd in range(2):
            pl.when(r % 2 == odd)(lambda odd=odd: pass_on(odd))

    def stage2_z(r, q):
        arrived(zf.at[q], zr_sem.at[r])
        for at in range(0, HALF, 16):
            rows = pl.ds(at, 16)
            encode(fwd_out.at[r, rows], t_far[q, mine(at)] + decode(zf.at[q, 0, rows]))
        c_fwd(r, 0, 1).start()
        c_fwd(r, 1, 1).start()
        for rel in range(3):
            for at in range(0, HALF, 16):
                t[r, rel, mine(at)] = t[r, rel, mine(at)] + decode(zf.at[q, 1 + rel, pl.ds(at, 16)])

    def stage3_y(r):
        arrived(rcv.at[r], rcv_sem.at[r])
        for at in range(0, SET, 16):
            rows = pl.ds(at, 16)
            t[r, 2, rows] = t[r, 2, rows] + decode(rcv.at[r, 0, rows]) + decode(rcv.at[r, 1, rows])
        for at in range(0, HALF, 16):
            encode(zr_out.at[r, pl.ds(at, 16)], t[r, 2, others(at)])
        c_zr(r).start()

    def stage3_z(r, q):
        arrived(fwd.at[r, pl.ds(0, HALF)], fwd_sem.at[r])
        for side in range(2):
            for at in range(0, HALF, 16):
                rows = pl.ds(at, 16)
                value = t[r, side, mine(at)]
                if (at >= 48) == (side == 1):
                    value = value + decode(fwd.at[r, rows])
                encode(rcv_out.at[r, side, rows], value)
            c_rcv(r, side, 1).start()

    def exchange(r):
        for d in range(1, 5):
            encode(xr_out.at[r, d - 1], f[r, d])
            if d < 4:
                c_xr(r, d).start()

        @pl.when(zh == 0)
        def _():
            c_xr(r, 4).start()

    def stage4_y(r):
        arrived(zr.at[r], zr_sem.at[r])
        own_rows = pl.ds(pl.multiple_of(HALF * zh, 16), 64)
        theirs = pl.ds(pl.multiple_of(16 * zh, 16), 64)
        f[r, 0:4] = (t[r, 2, own_rows] + decode(zr.at[r, theirs])).reshape(4, 16, QN)
        f[r, 4] = t[r, 2, pl.ds(64, 16)] + decode(zr.at[r, pl.ds(64, 16)])
        exchange(r)

    def stage4_z(r, q):
        arrived(rcv.at[r, :, pl.ds(0, HALF)], rcv_sem.at[r])
        for at in range(0, HALF, 16):
            rows = pl.ds(at, 16)
            t[r, 2, rows] = t[r, 2, mine(at)] + decode(rcv.at[r, 0, rows]) + decode(rcv.at[r, 1, rows])
        f[r, 0:4] = t[r, 2, pl.ds(pl.multiple_of(16 * zh, 16), 64)].reshape(4, 16, QN)
        f[r, 4] = t[r, 2, pl.ds(64, 16)]
        exchange(r)

    def stage5(r):
        @pl.when(zh == 0)
        def _():
            arrived(xr.at[r, 0:3], xr_sem.at[r])

        @pl.when(zh == 1)
        def _():
            arrived(xr.at[r], xr_sem.at[r])

        s, n = r // RN, r % RN
        columns = pl.ds(pl.multiple_of(n * QN, QN), QN)

        def place(block, b, swap):
            for i in range(4):
                for j in range(4):
                    p, q = (j, i) if swap else (i, j)
                    at = (p // 2) * 8 + (q // 2) * 4 + (p % 2) * 2 + q % 2
                    lad_ref[s, pl.ds(i * 32 + b * 4 + j, 1), columns] = block(at)

        def from_f(d):
            return lambda at: f[r, d, pl.ds(at, 1)]

        def from_xr(d):
            value = decode(xr.at[r, d - 1])
            return lambda at: value[at : at + 1]

        def at_of(p, q):
            return (p // 2) * 8 + (q // 2) * 4 + (p % 2) * 2 + q % 2

        for i in range(4):
            for j in range(4):
                lad_ref[s, pl.ds(i * 32 + col * 4 + j, 1), columns] = (
                    f[r, 0, pl.ds(at_of(i, j), 1)] + f[r, 0, pl.ds(at_of(j, i), 1)]
                )
        for d in range(1, 4):
            place(from_f(d), (col + d) % NB, False)
            place(from_xr(d), (col + NB - d) % NB, True)

        @pl.when(zh == 0)
        def _():
            place(from_f(4), (col + 4) % NB, False)

        @pl.when(zh == 1)
        def _():
            place(from_xr(4), (col + 4) % NB, True)

        @pl.when(n == RN - 1)
        def _():
            write(s).start()

    def write(s):
        return pltpu.make_async_copy(lad_ref.at[s], out_hbm.at[s], own_sem.at[s])

    stages = ((stage2_y, stage2_z), (stage3_y, stage3_z), (stage4_y, stage4_z), (stage5, None))

    send_own_z(0)
    send_own_x(0)
    pass_z(0)
    cz(2, own).start()
    send_own_z(1)
    pass_x(0, 0)
    straight(2)
    send_own_x(1)
    cx(0, lefts[1], 0, 1).wait_recv()
    ct(0, lefts[1]).start()
    cx(0, rights[1], 1, 1).wait_recv()
    ct(0, rights[1]).start()
    far_arrived(0, 0)
    cz(0, fars[0], 6).start()
    ct(0, fars[0]).start()
    straight_across(2, 0, own_z)
    straight_pass(2)
    pass_z(1)
    straight_across(0, 6, fars[1])
    load.wait()
    end_twin(0)

    def gather3():
        pass_x(1, 0)

    def gather4():
        straight_far(2)

    def gather6():
        straight_across(2, 1, lefts[1])
        pass_x(1, 1)
        straight_across(2, 2, rights[1])

    def gather7():
        pass_far(1)
        straight_across(2, 3, fars[1])

    def gather8():
        end_twin(1)
        end_twin(2)

    def step(it, carry):
        for when, hook in ((1, gather3), (2, gather4), (4, gather6), (6, gather7), (8, gather8)):
            pl.when(it == when)(hook)

        @pl.when(it < RN)
        def _():
            stage1(it, [(0, e_l)])

        @pl.when((it >= RN + GAP) & (it < ROUNDS + GAP))
        def _():
            one = it < 2 * RN + GAP
            stage1(it - GAP, [(1, jnp.where(one, e_ff, e_fs)), (2, jnp.where(one, e_sf, e_ss))])

        for n in range(4):
            stage, zstage = stages[n]
            lone_r, r, z_r = it - LONE_LAGS[n], it - GAP - LAGS[n], it - GAP - Z_LAGS[n]
            is_lone = (lone_r >= 0) & (lone_r < RN)
            is_pair = (r >= RN) & (r < ROUNDS)
            if zstage is None:
                pl.when(is_lone)(lambda: stage(lone_r))
                pl.when(is_pair)(lambda: stage(r))
            else:
                pl.when(is_lone)(lambda: stage(lone_r))
                pl.when(is_pair & jnp.logical_not(zfirst_of(r)))(lambda: stage(r))
                pl.when(zfirst_of(z_r))(lambda: zstage(z_r, (z_r - RN) // 2))

        return carry

    lax.fori_loop(0, ROUNDS + GAP + LAGS[-1], step, 0)

    end_sends()
    for slot in range(3):
        write(slot).wait()


def ladder_call(tile_pairs, amplitudes, integrals):
    dma = pltpu.SemaphoreType.DMA
    return pl.pallas_call(
        kernel,
        out_shape=jax.ShapeDtypeStruct((3, 128, 1024), jnp.float32),
        in_specs=[
            pl.BlockSpec(memory_space=pltpu.VMEM),
            pl.BlockSpec(memory_space=pl.ANY),
            pl.BlockSpec(memory_space=pl.ANY),
        ],
        out_specs=pl.BlockSpec(memory_space=pl.ANY),
        scratch_shapes=[
            pltpu.VMEM((3, NB, 2, 64, 2048), jnp.bfloat16),
            pltpu.VMEM((5, 2048, 1024), jnp.bfloat16),
            pltpu.VMEM((NB, 2, NB, 8, QN), jnp.float32),
            pltpu.VMEM((ROUNDS, 3, SET, QN), jnp.float32),
            pltpu.VMEM((ZROUNDS, SET, QN), jnp.float32),
            pltpu.VMEM((ROUNDS, SET, WIDE), jnp.bfloat16),
            pltpu.VMEM((ROUNDS, SET, WIDE), jnp.bfloat16),
            pltpu.VMEM((ROUNDS, 2, SET, WIDE), jnp.bfloat16),
            pltpu.VMEM((ROUNDS, 2, SET, WIDE), jnp.bfloat16),
            pltpu.VMEM((ZROUNDS, 4, HALF, WIDE), jnp.bfloat16),
            pltpu.VMEM((ZROUNDS, 4, HALF, WIDE), jnp.bfloat16),
            pltpu.VMEM((ROUNDS, HALF, WIDE), jnp.bfloat16),
            pltpu.VMEM((ROUNDS, HALF, WIDE), jnp.bfloat16),
            pltpu.VMEM((ROUNDS, 5, 16, QN), jnp.float32),
            pltpu.VMEM((ROUNDS, 4, 16, WIDE), jnp.bfloat16),
            pltpu.VMEM((ROUNDS, 4, 16, WIDE), jnp.bfloat16),
            pltpu.VMEM((3, 128, 1024), jnp.float32),
            pltpu.VMEM((3, 64, 2048), jnp.bfloat16),
            dma,
            dma((7,)),
            dma((3, 2, 2)),
            dma((3, 2)),
            dma((3,)),
            dma((ROUNDS,)),
            dma((ROUNDS,)),
            dma((ROUNDS,)),
            dma((ROUNDS,)),
            dma((11,)),
            dma((4,)),
        ],
        compiler_params=pltpu.CompilerParams(
            collective_id=0, has_side_effects=True, vmem_limit_bytes=60 << 20
        ),
        cost_estimate=pl.CostEstimate(flops=21_474_836_480, bytes_accessed=24 << 20, transcendentals=0),
    )(tile_pairs, amplitudes, integrals)


def finish(tp_ref, lad_hbm, drv_hbm, occ_ref, virt_ref, res_hbm, upd_hbm, lad_ref, drv_ref, res_ref, upd_ref, sem):
    row, col = lax.axis_index("row"), lax.axis_index("col")
    lone = read_pairs(tp_ref)[2]
    parts = [(tile, pl.ds(64 * half, 64)) for tile in range(3) for half in range(2)]
    reads = []
    for n, (tile, rows) in enumerate(parts):
        slot = jnp.where(lone == tile, 0, 1 + tile - jnp.where(lone < tile, 1, 0))
        reads.append(pltpu.make_async_copy(lad_hbm.at[slot, rows], lad_ref.at[tile, rows], sem.at[0, n]))
        reads.append(pltpu.make_async_copy(drv_hbm.at[tile, rows], drv_ref.at[tile, rows], sem.at[1, n]))
    for c in reads:
        c.start()
    lanes = occ_ref[...].reshape(1, 32)
    across = lax.broadcasted_iota(jnp.int32, (32, 32), 1)
    eye = lax.broadcasted_iota(jnp.int32, (32, 32), 0) == across
    second = jnp.sum(jnp.where(eye, jnp.broadcast_to(lanes, (32, 32)), 0.0), axis=1, keepdims=True)
    place = lax.broadcasted_iota(jnp.int32, (1, 128), 1)
    sums = []
    for i in range(4):
        here = jnp.sum(jnp.where(across[:1] == col * 4 + i, lanes, 0.0), axis=1, keepdims=True)
        sums.append(jnp.broadcast_to(here + second, (32, 128)))
    for tile in range(3):
        inner, outer = virt_ref[tile, 1:2, :], virt_ref[tile, 0:1, :]
        for c in range(8):
            lead = jnp.sum(jnp.where(place == row * 8 + c, outer, 0.0), axis=1, keepdims=True)
            virtual_pair = lead + inner
            for i in range(4):
                upd_ref[tile, pl.ds(i * 32, 32), pl.ds(c * 128, 128)] = 1.0 / (sums[i] - virtual_pair)
    writes = []
    for n, (tile, rows) in enumerate(parts):
        reads[2 * n].wait()
        reads[2 * n + 1].wait()
        residual = drv_ref[tile, rows].astype(jnp.float32) + lad_ref[tile, rows]
        res_ref[tile, rows] = residual
        upd_ref[tile, rows] = residual * upd_ref[tile, rows]
        writes.append(pltpu.make_async_copy(res_ref.at[tile, rows], res_hbm.at[tile, rows], sem.at[2, n]))
        writes.append(pltpu.make_async_copy(upd_ref.at[tile, rows], upd_hbm.at[tile, rows], sem.at[3, n]))
        writes[-2].start()
        writes[-1].start()
    for c in writes:
        c.wait()


def body(amplitudes, integrals, tile_pairs, driving, occupied_energy, virtual_energy):
    pairs = tile_pairs.T
    ladder = ladder_call(pairs, amplitudes, integrals)
    vmem, anywhere = pl.BlockSpec(memory_space=pltpu.VMEM), pl.BlockSpec(memory_space=pl.ANY)
    out = jax.ShapeDtypeStruct(driving.shape, jnp.float32)
    held = pltpu.VMEM(driving.shape, jnp.float32)
    return pl.pallas_call(
        finish,
        out_shape=[out, out],
        in_specs=[vmem, anywhere, anywhere, vmem, vmem],
        out_specs=[anywhere, anywhere],
        scratch_shapes=[held, pltpu.VMEM(driving.shape, jnp.bfloat16), held, held, pltpu.SemaphoreType.DMA((4, 6))],
        compiler_params=pltpu.CompilerParams(vmem_limit_bytes=60 << 20),
    )(pairs, ladder, driving, occupied_energy, virtual_energy)


def solution(mesh):
    return jax.shard_map(
        body,
        mesh=mesh,
        in_specs=(
            P(None, "row", "col"),
            P(None, "col", "row"),
            P(),
            P(None, "col", "row"),
            P(),
            P(),
        ),
        out_specs=(P(None, "col", "row"), P(None, "col", "row")),
        check_vma=False,
    )
```

```python
import functools

import jax
import jax.numpy as jnp
from jax import lax
from jax.experimental import pallas as pl
from jax.experimental.pallas import tpu as pltpu
from jax.sharding import PartitionSpec as P

MESH = pl.DeviceIdType.MESH
NB = 8
QN = 256
RN = 4
ROUNDS = 12
SET = 144
HALF = 80
WIDE = QN + QN // 2
LEVELS = 10
LONE_LAGS, LAGS, Z_LAGS = (2, 7, 10, 14), (1, 3, 5, 9), (3, 4, 6, 9)
ZROUNDS = 1
GAP = 4


def encode(ref, value):
    lead = value.astype(jnp.bfloat16)
    wide = lead.astype(jnp.float32)
    safe = jnp.where(jnp.abs(wide) < 1e-36, 1.0, wide)
    steps = jnp.round((value - wide) * pl.reciprocal(safe, approx=True) * (256.0 * LEVELS))
    steps = jnp.clip(steps, -LEVELS, LEVELS)
    half = QN // 2
    ref[:, :QN] = lead
    ref[:, QN:] = (steps[:, :half] * (2 * LEVELS + 1) + steps[:, half:]).astype(jnp.bfloat16)


def decode(ref):
    wide = ref[:, :QN].astype(jnp.float32)
    code = ref[:, QN:].astype(jnp.float32)
    first = jnp.round(code * (1.0 / (2 * LEVELS + 1)))
    second = code - first * (2 * LEVELS + 1)
    return wide + wide * (jnp.concatenate([first, second], axis=1) * (1.0 / (256.0 * LEVELS)))


def read_pairs(tp_ref):
    pairs = tp_ref[...]
    src = [pairs[0, e] for e in range(5)]
    dst = [pairs[1, e] for e in range(5)]
    counts = [sum((src[e] == v).astype(jnp.int32) for e in range(5)) for v in range(3)]
    return src, dst, jnp.where(counts[0] == 1, 0, jnp.where(counts[1] == 1, 1, 2))


def kernel(
    tp_ref, amp_hbm, int_hbm, out_hbm,
    g, wt, s_buf, t, t_far, fwd_out, fwd, rcv_out, rcv, zf_out, zf, zr_out, zr, f, xr_out, xr, lad_ref, amp_ref,
    int_sem, z_sem, x_sem, f_sem, t_sem, fwd_sem, rcv_sem, zr_sem, xr_sem, send_sem, own_sem,
):
    row, col = lax.axis_index("row"), lax.axis_index("col")
    x, zl, k = row // 4, (row // 2) % 2, row % 2
    zh, y = col // 4, col % 4

    def at_row(xx, zz, kk):
        return (xx * 4 + zz * 2 + kk, col)

    def at_col(cc):
        return (row, cc)

    xp, xm, xo = (x + 1) % 4, (x + 3) % 4, (x + 2) % 4
    yp, ym, yo = (y + 1) % 4, (y + 3) % 4, (y + 2) % 4
    right, left = at_row(xp, zl, k), at_row(xm, zl, k)
    zpart, twin = at_row(x, 1 - zl, k), at_row(x, zl, 1 - k)
    up, down = at_col(zh * 4 + yp), at_col(zh * 4 + ym)
    far = at_col((1 - zh) * 4 + y)

    load_own = pltpu.make_async_copy(amp_hbm, amp_ref, own_sem.at[3])
    load_own.start()

    barrier = pltpu.get_barrier_semaphore()
    partners = [right, left, zpart, twin] + [at_col((col + d) % NB) for d in range(1, NB)]
    for p in partners:
        pl.semaphore_signal(barrier, inc=1, device_id=p, device_id_type=MESH)
    load = pltpu.make_async_copy(int_hbm, wt, int_sem)
    load.start()

    src, dst, lone = read_pairs(tp_ref)
    first = jnp.where(lone == 0, 1, 0)
    second = jnp.where(lone == 2, 1, 2)

    def entry(a, b):
        found = jnp.int32(0)
        for e in range(1, 5):
            found = jnp.where((src[e] == a) & (dst[e] == b), e, found)
        return found

    e_l = entry(lone, lone)
    e_ff, e_sf = entry(first, first), entry(second, first)
    e_fs, e_ss = entry(first, second), entry(second, second)

    own = x * 2 + zl
    to = lax.broadcasted_iota(jnp.int32, (64, 64), 0)
    frm = lax.broadcasted_iota(jnp.int32, (64, 64), 1)
    block, mid, low = to // 8, (to // 2) % 2, to % 2
    distance = (block + NB - own) % NB
    direct = (distance < 4) | ((distance == 4) & (block >= 4))
    ilo, jlo = jnp.where(direct, mid, low), jnp.where(direct, low, mid)
    order64 = (frm == ilo * 32 + block * 4 + ((to // 4) % 2) * 2 + jlo).astype(jnp.bfloat16)
    load_own.wait()
    for s, tile in ((0, lone), (2, second), (1, first)):
        g[s, own, k] = jnp.dot(order64, amp_ref[tile], preferred_element_type=jnp.float32).astype(jnp.bfloat16)
    pl.semaphore_wait(barrier, len(partners))

    def rdma(ref_src, ref_dst, ss, rs, dev):
        return pltpu.make_async_remote_copy(
            src_ref=ref_src, dst_ref=ref_dst, send_sem=ss, recv_sem=rs, device_id=dev, device_id_type=MESH
        )

    def chip(xx, zz):
        return xx * 2 + zz

    def cz(s, a, i=0):
        return rdma(g.at[s, a, k], g.at[s, a, k], send_sem.at[0], z_sem.at[s + i], zpart)

    def cx(s, a, side, which):
        return rdma(g.at[s, a, k], g.at[s, a, k], send_sem.at[1], x_sem.at[s, side, which], right if side == 0 else left)

    def cf(s, a, side, which):
        part = g.at[s, a, k, pl.ds(32 * side, 32)]
        return rdma(part, part, send_sem.at[2], f_sem.at[s, which], right if side == 0 else left)

    def far_arrived(s, which):
        whole = g.at[s, fars[which], k]
        rdma(whole, whole, send_sem.at[2], f_sem.at[s, which], right).wait_recv()

    def ct(s, a):
        return rdma(g.at[s, a, k], g.at[s, a, k], send_sem.at[3], t_sem.at[s], twin)

    own_z = chip(x, 1 - zl)
    lefts, rights = (chip(xm, zl), chip(xm, 1 - zl)), (chip(xp, zl), chip(xp, 1 - zl))
    fars = (chip(xo, zl), chip(xo, 1 - zl))

    def send_own_z(s):
        cz(s, own).start()

    def send_own_x(s):
        cx(s, own, 0, 0).start()
        cx(s, own, 1, 0).start()
        ct(s, own).start()

    def pass_z(s):
        cz(s, own_z).wait_recv()
        cx(s, own_z, 0, 1).start()
        cx(s, own_z, 1, 1).start()
        ct(s, own_z).start()

    def pass_x(s, which):
        cx(s, lefts[which], 0, which).wait_recv()
        cf(s, lefts[which], 0, which).start()
        ct(s, lefts[which]).start()
        cx(s, rights[which], 1, which).wait_recv()
        cf(s, rights[which], 1, which).start()
        ct(s, rights[which]).start()

    def pass_far(s):
        for which in range(2):
            far_arrived(s, which)
            ct(s, fars[which]).start()

    def end_twin(s):
        half = g.at[s, :, 1 - k]
        rdma(half, half, send_sem.at[3], t_sem.at[s], twin).wait_recv()

    def straight(s):
        cx(s, own, 0, 0).start()
        cx(s, own, 1, 0).start()
        ct(s, own).start()

    def straight_pass(s):
        cx(s, lefts[0], 0, 0).wait_recv()
        cf(s, lefts[0], 0, 0).start()
        cx(s, rights[0], 1, 0).wait_recv()
        cf(s, rights[0], 1, 0).start()
        cz(s, lefts[0], 1).start()
        cz(s, rights[0], 2).start()
        ct(s, lefts[0]).start()
        ct(s, rights[0]).start()

    def straight_far(s):
        far_arrived(s, 0)
        cz(s, fars[0], 3).start()
        ct(s, fars[0]).start()

    def straight_across(s, i, a):
        cz(s, a, i).wait_recv()
        ct(s, a).start()

    def sent(ref, i):
        rdma(ref, ref, send_sem.at[i], z_sem.at[0], twin).wait_send()

    def end_sends():
        sent(g.at[0, 0:7, 0], 0)
        sent(g.at[0, 0:5], 1)
        sent(g.at[0, 0:2], 2)
        sent(g.at[:, :, 0], 3)
        sent(fwd_out.at[0 : ROUNDS - ZROUNDS], 4)
        sent(fwd_out.at[0:ZROUNDS, pl.ds(0, HALF)], 5)
        sent(rcv_out.at[0 : ROUNDS - ZROUNDS], 6)
        sent(rcv_out.at[0:ZROUNDS, :, pl.ds(0, HALF)], 7)
        sent(zr.at[0 : ROUNDS - ZROUNDS], 8)
        sent(zf_out, 9)

        @pl.when(zh == 0)
        def _():
            sent(xr_out, 10)

        @pl.when(zh == 1)
        def _():
            sent(xr_out.at[:, 0:3], 10)

    def c_fwd(r, side, zfirst, odd=0):
        if zfirst:
            rows = pl.ds(48 * side, 48 - 16 * side)
        else:
            rows = pl.ds(0, HALF) if side != odd else pl.ds(HALF, SET - HALF)
        return rdma(
            fwd_out.at[r, rows], fwd.at[r, rows], send_sem.at[4 + zfirst], fwd_sem.at[r], up if side == 0 else down
        )

    def c_rcv(r, side, zfirst):
        rows = pl.ds(0, HALF if zfirst else SET)
        return rdma(
            rcv_out.at[r, side, rows], rcv.at[r, side, rows],
            send_sem.at[6 + zfirst], rcv_sem.at[r], up if side == 0 else down,
        )

    def arrived(ref, sem):
        rdma(ref, ref, send_sem.at[4], sem, twin).wait_recv()

    def c_zr(r):
        return rdma(zr_out.at[r], zr.at[r], send_sem.at[8], zr_sem.at[r], far)

    def c_zf(q, r):
        return rdma(zf_out.at[q], zf.at[q], send_sem.at[9], zr_sem.at[r], far)

    def c_xr(r, d):
        return rdma(xr_out.at[r, d - 1], xr.at[r, d - 1], send_sem.at[10], xr_sem.at[r], at_col((col + d) % NB))

    def zfirst_of(r):
        return (r > RN) & (r < RN + 2 * ZROUNDS) & (r % 2 == 1)

    def both(stage, zstage):
        def run(r):
            pl.when(jnp.logical_not(zfirst_of(r)))(lambda: stage(r))
            pl.when(zfirst_of(r))(lambda: zstage(r, (r - RN) // 2))

        return run

    def mine(at):
        return pl.ds(pl.multiple_of(64 * zh + at, 16), 16)

    def others(at):
        return pl.ds(pl.multiple_of(64 * (1 - zh) + at, 16), 16)

    def make_block(c, d):
        b = (c + d) % NB
        direct = s_buf[c, :, b]
        if d == 0:
            return direct
        other = s_buf[b, :, c]
        mirrored = jnp.stack(
            [
                jnp.concatenate([other[0, :4], other[1, :4]], axis=0),
                jnp.concatenate([other[0, 4:], other[1, 4:]], axis=0),
            ]
        )
        return direct + mirrored

    def stage1(r, pairs):
        n = r % RN
        columns = pl.ds(pl.multiple_of(n * QN, QN), QN)
        for m in range(4):
            total = None
            for slot, e in pairs:
                lhs = g[slot, 2 * m : 2 * m + 2].reshape(256, 2048)
                part = jnp.dot(lhs, wt[e, :, columns], preferred_element_type=jnp.float32)
                total = part if total is None else total + part
            s_buf[2 * m : 2 * m + 2] = total.reshape(2, 2, 8, 8, QN)
        def form(store, after_far=lambda: None):
            for rel, yy in enumerate((yo, yp, ym, y)):
                at = 0
                for zz in range(2):
                    for d in range(5 - zz):
                        store(rel, pl.ds(at, 16), make_block(zz * 4 + yy, d).reshape(16, QN))
                        at += 16
                if rel == 0:
                    after_far()

        def form_y(r):
            def store(rel, rows, value):
                if rel == 0:
                    encode(fwd_out.at[r, rows], value)
                else:
                    t[r, rel - 1, rows] = value

            def send():
                for odd in range(2):
                    @pl.when(r % 2 == odd)
                    def _(odd=odd):
                        c_fwd(r, 0, 0, odd).start()
                        c_fwd(r, 1, 0, odd).start()

            form(store, send)

        def form_z(r, q):
            def store(rel, rows, value):
                if rel == 0:
                    t_far[q, rows] = value
                else:
                    t[r, rel - 1, rows] = value

            form(store)
            for at in range(0, HALF, 16):
                encode(zf_out.at[q, 0, pl.ds(at, 16)], t_far[q, others(at)])
                for rel in range(3):
                    encode(zf_out.at[q, 1 + rel, pl.ds(at, 16)], t[r, rel, others(at)])
            c_zf(q, r).start()

        if len(pairs) == 1:
            form_y(r)
        else:
            both(form_y, form_z)(r)

    def stage2_y(r):
        arrived(fwd.at[r], fwd_sem.at[r])

        def pass_on(odd):
            for side in range(2):
                for at in range(0, SET, 16):
                    rows = pl.ds(at, 16)
                    value = t[r, side, rows]
                    if (at < HALF) == (side != odd):
                        value = value + decode(fwd.at[r, rows])
                    encode(rcv_out.at[r, side, rows], value)
                c_rcv(r, side, 0).start()

        for odd in range(2):
            pl.when(r % 2 == odd)(lambda odd=odd: pass_on(odd))

    def stage2_z(r, q):
        arrived(zf.at[q], zr_sem.at[r])
        for at in range(0, HALF, 16):
            rows = pl.ds(at, 16)
            encode(fwd_out.at[r, rows], t_far[q, mine(at)] + decode(zf.at[q, 0, rows]))
        c_fwd(r, 0, 1).start()
        c_fwd(r, 1, 1).start()
        for rel in range(3):
            for at in range(0, HALF, 16):
                t[r, rel, mine(at)] = t[r, rel, mine(at)] + decode(zf.at[q, 1 + rel, pl.ds(at, 16)])

    def stage3_y(r):
        arrived(rcv.at[r], rcv_sem.at[r])
        for at in range(0, SET, 16):
            rows = pl.ds(at, 16)
            t[r, 2, rows] = t[r, 2, rows] + decode(rcv.at[r, 0, rows]) + decode(rcv.at[r, 1, rows])
        for at in range(0, HALF, 16):
            encode(zr_out.at[r, pl.ds(at, 16)], t[r, 2, others(at)])
        c_zr(r).start()

    def stage3_z(r, q):
        arrived(fwd.at[r, pl.ds(0, HALF)], fwd_sem.at[r])
        for side in range(2):
            for at in range(0, HALF, 16):
                rows = pl.ds(at, 16)
                value = t[r, side, mine(at)]
                if (at >= 48) == (side == 1):
                    value = value + decode(fwd.at[r, rows])
                encode(rcv_out.at[r, side, rows], value)
            c_rcv(r, side, 1).start()

    def exchange(r):
        for d in range(1, 5):
            encode(xr_out.at[r, d - 1], f[r, d])
            if d < 4:
                c_xr(r, d).start()

        @pl.when(zh == 0)
        def _():
            c_xr(r, 4).start()

    def stage4_y(r):
        arrived(zr.at[r], zr_sem.at[r])
        own_rows = pl.ds(pl.multiple_of(HALF * zh, 16), 64)
        theirs = pl.ds(pl.multiple_of(16 * zh, 16), 64)
        f[r, 0:4] = (t[r, 2, own_rows] + decode(zr.at[r, theirs])).reshape(4, 16, QN)
        f[r, 4] = t[r, 2, pl.ds(64, 16)] + decode(zr.at[r, pl.ds(64, 16)])
        exchange(r)

    def stage4_z(r, q):
        arrived(rcv.at[r, :, pl.ds(0, HALF)], rcv_sem.at[r])
        for at in range(0, HALF, 16):
            rows = pl.ds(at, 16)
            t[r, 2, rows] = t[r, 2, mine(at)] + decode(rcv.at[r, 0, rows]) + decode(rcv.at[r, 1, rows])
        f[r, 0:4] = t[r, 2, pl.ds(pl.multiple_of(16 * zh, 16), 64)].reshape(4, 16, QN)
        f[r, 4] = t[r, 2, pl.ds(64, 16)]
        exchange(r)

    def stage5(r):
        @pl.when(zh == 0)
        def _():
            arrived(xr.at[r, 0:3], xr_sem.at[r])

        @pl.when(zh == 1)
        def _():
            arrived(xr.at[r], xr_sem.at[r])

        s, n = r // RN, r % RN
        columns = pl.ds(pl.multiple_of(n * QN, QN), QN)

        def place(block, b, swap):
            for i in range(4):
                for j in range(4):
                    p, q = (j, i) if swap else (i, j)
                    at = (p // 2) * 8 + (q // 2) * 4 + (p % 2) * 2 + q % 2
                    lad_ref[s, pl.ds(i * 32 + b * 4 + j, 1), columns] = block(at)

        def from_f(d):
            return lambda at: f[r, d, pl.ds(at, 1)]

        def from_xr(d):
            value = decode(xr.at[r, d - 1])
            return lambda at: value[at : at + 1]

        def at_of(p, q):
            return (p // 2) * 8 + (q // 2) * 4 + (p % 2) * 2 + q % 2

        for i in range(4):
            for j in range(4):
                lad_ref[s, pl.ds(i * 32 + col * 4 + j, 1), columns] = (
                    f[r, 0, pl.ds(at_of(i, j), 1)] + f[r, 0, pl.ds(at_of(j, i), 1)]
                )
        for d in range(1, 4):
            place(from_f(d), (col + d) % NB, False)
            place(from_xr(d), (col + NB - d) % NB, True)

        @pl.when(zh == 0)
        def _():
            place(from_f(4), (col + 4) % NB, False)

        @pl.when(zh == 1)
        def _():
            place(from_xr(4), (col + 4) % NB, True)

        @pl.when(n == RN - 1)
        def _():
            write(s).start()

    def write(s):
        return pltpu.make_async_copy(lad_ref.at[s], out_hbm.at[s], own_sem.at[s])

    stages = ((stage2_y, stage2_z), (stage3_y, stage3_z), (stage4_y, stage4_z), (stage5, None))

    send_own_z(0)
    send_own_x(0)
    pass_z(0)
    cz(2, own).start()
    send_own_z(1)
    pass_x(0, 0)
    straight(2)
    send_own_x(1)
    cx(0, lefts[1], 0, 1).wait_recv()
    ct(0, lefts[1]).start()
    cx(0, rights[1], 1, 1).wait_recv()
    ct(0, rights[1]).start()
    far_arrived(0, 0)
    cz(0, fars[0], 6).start()
    ct(0, fars[0]).start()
    straight_across(2, 0, own_z)
    straight_pass(2)
    pass_z(1)
    straight_across(0, 6, fars[1])
    load.wait()
    end_twin(0)

    def gather3():
        pass_x(1, 0)

    def gather4():
        straight_far(2)

    def gather6():
        straight_across(2, 1, lefts[1])
        pass_x(1, 1)
        straight_across(2, 2, rights[1])

    def gather7():
        pass_far(1)
        straight_across(2, 3, fars[1])

    def gather8():
        end_twin(1)
        end_twin(2)

    def step(it, carry):
        for when, hook in ((1, gather3), (2, gather4), (4, gather6), (6, gather7), (8, gather8)):
            pl.when(it == when)(hook)

        @pl.when(it < RN)
        def _():
            stage1(it, [(0, e_l)])

        @pl.when((it >= RN + GAP) & (it < ROUNDS + GAP))
        def _():
            one = it < 2 * RN + GAP
            stage1(it - GAP, [(1, jnp.where(one, e_ff, e_fs)), (2, jnp.where(one, e_sf, e_ss))])

        for n in range(4):
            stage, zstage = stages[n]
            lone_r, r, z_r = it - LONE_LAGS[n], it - GAP - LAGS[n], it - GAP - Z_LAGS[n]
            is_lone = (lone_r >= 0) & (lone_r < RN)
            is_pair = (r >= RN) & (r < ROUNDS)
            if zstage is None:
                pl.when(is_lone)(lambda: stage(lone_r))
                pl.when(is_pair)(lambda: stage(r))
            else:
                pl.when(is_lone)(lambda: stage(lone_r))
                pl.when(is_pair & jnp.logical_not(zfirst_of(r)))(lambda: stage(r))
                pl.when(zfirst_of(z_r))(lambda: zstage(z_r, (z_r - RN) // 2))

        return carry

    lax.fori_loop(0, ROUNDS + GAP + LAGS[-1], step, 0)

    end_sends()
    for slot in range(3):
        write(slot).wait()


def ladder_call(tile_pairs, amplitudes, integrals):
    dma = pltpu.SemaphoreType.DMA
    return pl.pallas_call(
        kernel,
        out_shape=jax.ShapeDtypeStruct((3, 128, 1024), jnp.float32),
        in_specs=[
            pl.BlockSpec(memory_space=pltpu.VMEM),
            pl.BlockSpec(memory_space=pl.ANY),
            pl.BlockSpec(memory_space=pl.ANY),
        ],
        out_specs=pl.BlockSpec(memory_space=pl.ANY),
        scratch_shapes=[
            pltpu.VMEM((3, NB, 2, 64, 2048), jnp.bfloat16),
            pltpu.VMEM((5, 2048, 1024), jnp.bfloat16),
            pltpu.VMEM((NB, 2, NB, 8, QN), jnp.float32),
            pltpu.VMEM((ROUNDS, 3, SET, QN), jnp.float32),
            pltpu.VMEM((ZROUNDS, SET, QN), jnp.float32),
            pltpu.VMEM((ROUNDS, SET, WIDE), jnp.bfloat16),
            pltpu.VMEM((ROUNDS, SET, WIDE), jnp.bfloat16),
            pltpu.VMEM((ROUNDS, 2, SET, WIDE), jnp.bfloat16),
            pltpu.VMEM((ROUNDS, 2, SET, WIDE), jnp.bfloat16),
            pltpu.VMEM((ZROUNDS, 4, HALF, WIDE), jnp.bfloat16),
            pltpu.VMEM((ZROUNDS, 4, HALF, WIDE), jnp.bfloat16),
            pltpu.VMEM((ROUNDS, HALF, WIDE), jnp.bfloat16),
            pltpu.VMEM((ROUNDS, HALF, WIDE), jnp.bfloat16),
            pltpu.VMEM((ROUNDS, 5, 16, QN), jnp.float32),
            pltpu.VMEM((ROUNDS, 4, 16, WIDE), jnp.bfloat16),
            pltpu.VMEM((ROUNDS, 4, 16, WIDE), jnp.bfloat16),
            pltpu.VMEM((3, 128, 1024), jnp.float32),
            pltpu.VMEM((3, 64, 2048), jnp.bfloat16),
            dma,
            dma((7,)),
            dma((3, 2, 2)),
            dma((3, 2)),
            dma((3,)),
            dma((ROUNDS,)),
            dma((ROUNDS,)),
            dma((ROUNDS,)),
            dma((ROUNDS,)),
            dma((11,)),
            dma((4,)),
        ],
        compiler_params=pltpu.CompilerParams(
            collective_id=0, has_side_effects=True, vmem_limit_bytes=60 << 20
        ),
        cost_estimate=pl.CostEstimate(flops=21_474_836_480, bytes_accessed=24 << 20, transcendentals=0),
    )(tile_pairs, amplitudes, integrals)


def finish(tp_ref, lad_hbm, drv_hbm, occ_ref, virt_ref, res_hbm, upd_hbm, lad_ref, drv_ref, res_ref, upd_ref, sem):
    row, col = lax.axis_index("row"), lax.axis_index("col")
    lone = read_pairs(tp_ref)[2]
    parts = [(tile, pl.ds(64 * half, 64)) for tile in range(3) for half in range(2)]
    reads = []
    for n, (tile, rows) in enumerate(parts):
        slot = jnp.where(lone == tile, 0, 1 + tile - jnp.where(lone < tile, 1, 0))
        reads.append(pltpu.make_async_copy(lad_hbm.at[slot, rows], lad_ref.at[tile, rows], sem.at[0, n]))
        reads.append(pltpu.make_async_copy(drv_hbm.at[tile, rows], drv_ref.at[tile, rows], sem.at[1, n]))
    for c in reads:
        c.start()
    lanes = occ_ref[...].reshape(1, 32)
    across = lax.broadcasted_iota(jnp.int32, (32, 32), 1)
    eye = lax.broadcasted_iota(jnp.int32, (32, 32), 0) == across
    second = jnp.sum(jnp.where(eye, jnp.broadcast_to(lanes, (32, 32)), 0.0), axis=1, keepdims=True)
    place = lax.broadcasted_iota(jnp.int32, (1, 128), 1)
    sums = []
    for i in range(4):
        here = jnp.sum(jnp.where(across[:1] == col * 4 + i, lanes, 0.0), axis=1, keepdims=True)
        sums.append(jnp.broadcast_to(here + second, (32, 128)))
    for tile in range(3):
        inner, outer = virt_ref[tile, 1:2, :], virt_ref[tile, 0:1, :]
        for c in range(8):
            lead = jnp.sum(jnp.where(place == row * 8 + c, outer, 0.0), axis=1, keepdims=True)
            virtual_pair = lead + inner
            for i in range(4):
                upd_ref[tile, pl.ds(i * 32, 32), pl.ds(c * 128, 128)] = 1.0 / (sums[i] - virtual_pair)
    writes = []
    for n, (tile, rows) in enumerate(parts):
        reads[2 * n].wait()
        reads[2 * n + 1].wait()
        residual = drv_ref[tile, rows].astype(jnp.float32) + lad_ref[tile, rows]
        res_ref[tile, rows] = residual
        upd_ref[tile, rows] = residual * upd_ref[tile, rows]
        writes.append(pltpu.make_async_copy(res_ref.at[tile, rows], res_hbm.at[tile, rows], sem.at[2, n]))
        writes.append(pltpu.make_async_copy(upd_ref.at[tile, rows], upd_hbm.at[tile, rows], sem.at[3, n]))
        writes[-2].start()
        writes[-1].start()
    for c in writes:
        c.wait()


def body(amplitudes, integrals, tile_pairs, driving, occupied_energy, virtual_energy):
    pairs = tile_pairs.T
    ladder = ladder_call(pairs, amplitudes, integrals)
    vmem, anywhere = pl.BlockSpec(memory_space=pltpu.VMEM), pl.BlockSpec(memory_space=pl.ANY)
    out = jax.ShapeDtypeStruct(driving.shape, jnp.float32)
    held = pltpu.VMEM(driving.shape, jnp.float32)
    return pl.pallas_call(
        finish,
        out_shape=[out, out],
        in_specs=[vmem, anywhere, anywhere, vmem, vmem],
        out_specs=[anywhere, anywhere],
        scratch_shapes=[held, pltpu.VMEM(driving.shape, jnp.bfloat16), held, held, pltpu.SemaphoreType.DMA((4, 6))],
        compiler_params=pltpu.CompilerParams(vmem_limit_bytes=60 << 20),
    )(pairs, ladder, driving, occupied_energy, virtual_energy)


def solution(mesh):
    return jax.shard_map(
        body,
        mesh=mesh,
        in_specs=(
            P(None, "row", "col"),
            P(None, "col", "row"),
            P(),
            P(None, "col", "row"),
            P(),
            P(),
        ),
        out_specs=(P(None, "col", "row"), P(None, "col", "row")),
        check_vma=False,
    )
```
